128 devices in a mesh: seq: 64 (over x, y_lo, z, core), dp: 2 (over y_hi).
Axes of the slice: x: 4, y: 4 (y_hi: 2, y_lo: 2; y = y_hi * 2 + y_lo), z: 4, core: 2. Of those that a mesh axis runs over, the one named last changes fastest.
Arguments:
- inputs: float32 [2, 32, 524288], P('dp', None, 'seq'), may hold values from -6 to 6
- grad_out: float32 [2, 32, 524288], P('dp', None, 'seq'), may hold values from -6 to 6
- filters: float32 [32, 524288], P(None, 'seq'), may hold values from -6 to 6
- skip: float32 [32], replicated, may hold values from 0.5 to 1.5
Outputs:
- grad_in: float32 [2, 32, 524288], P('dp', None, 'seq')
- filter_grad: float32 [32, 524288], P(None, 'seq')
The draws below stay inside these ranges and needn't reach their ends.
All inputs are finite; a program needn't handle non-finite values.
Results may differ from the reference program's by a relative error of at most 0.000098.
Values sent between devices are 32-bit elements; how exact they have to be, the bound alone decides.
A program may use at most 192 MiB of HBM per device.

```python
import math
import jax
import jax.numpy as jnp
from jax import lax

CHANNELS = 32
BATCH = 2
SEQ_LEN = 524288
FFT_LEN = 1048576


def block_scale(stream_key, shape, split, least, top_value):
    loudness = 1.0
    for dim, parts in split:
        heights = jax.random.uniform(jax.random.fold_in(jax.random.fold_in(stream_key, 6), dim), (parts,), jnp.float32, least / len(split), top_value / len(split))
        loudness = loudness * jnp.repeat(jnp.exp(heights), shape[dim] // parts).reshape((-1,) + (1,) * (len(shape) - 1 - dim))
    return loudness


def scatter_about(own_key, shape, deviation, bound, split=(), dtype=jnp.bfloat16):
    array = deviation * jax.random.normal(own_key, shape, jnp.float32)
    if split:
        array = array * block_scale(own_key, shape, split, -0.22, 0.18)
    return jnp.clip(array, -bound, bound).astype(dtype)


def setup_inputs(seed: int = 0) -> dict:
    seeds = jax.random.split(jax.random.key(seed), 5)
    inputs = scatter_about(seeds[0], (BATCH, CHANNELS, SEQ_LEN), 1.0, 6.0, ((0, 2), (2, 64)), jnp.float32)
    grad_out = scatter_about(seeds[1], (BATCH, CHANNELS, SEQ_LEN), 1.0, 6.0, ((0, 2), (2, 64)), jnp.float32)
    filters = scatter_about(seeds[2], (CHANNELS, SEQ_LEN), 1.0, 6.0, ((1, 64),), jnp.float32)
    skip = jnp.clip(jax.random.uniform(seeds[3], (CHANNELS,), jnp.float32, 0.5, 1.5), 0.5, 1.5)
    return dict(inputs=inputs, grad_out=grad_out, filters=filters, skip=skip)


def reference(inputs, grad_out, filters, skip):
    factor = 1.0 / math.sqrt(SEQ_LEN)

    def per_channel(operands):
        chan_in, chan_grad, chan_filter, chan_skip = operands
        in_spec = jnp.fft.fft(chan_in, n=FFT_LEN, axis=-1)
        grad_spec = jnp.fft.fft(chan_grad, n=FFT_LEN, axis=-1)
        filter_spec = jnp.fft.fft(chan_filter, n=FFT_LEN)
        input_cross = grad_spec * jnp.conj(filter_spec)[None, :]
        filter_cross = lax.optimization_barrier(jnp.sum(grad_spec * jnp.conj(in_spec), axis=0))
        conv_in = jnp.real(jnp.fft.ifft(input_cross, axis=-1))[:, :SEQ_LEN]
        conv_filter = jnp.real(jnp.fft.ifft(filter_cross))[:SEQ_LEN]
        grad_part = factor * conv_in + chan_skip * chan_grad
        return (grad_part.astype(jnp.float32), (factor * conv_filter).astype(jnp.float32))
    moved_in = jnp.swapaxes(inputs, 0, 1)
    moved_grad = jnp.swapaxes(grad_out, 0, 1)
    grad_parts, filter_grad = lax.map(per_channel, (moved_in, moved_grad, filters, skip))
    return (jnp.swapaxes(grad_parts, 0, 1), filter_grad)
```

```python
import functools
import math

import jax
import jax.numpy as jnp
import ml_dtypes
import numpy as np
from jax import lax
from jax.experimental import pallas as pl
from jax.experimental.pallas import tpu as pltpu
from jax.sharding import PartitionSpec as P

MESH = pl.DeviceIdType.MESH
CHIPS = 32
ROWS = 16
COLS = 512
RAD = 128
LENGTH = CHIPS * 2 * ROWS * COLS
WIDE = 256


def two_parts(matrix):
    high = matrix.astype(ml_dtypes.bfloat16)
    low = (matrix - high.astype(np.float64)).astype(ml_dtypes.bfloat16)
    return high, low


def left_blocks(matrix):
    high, low = two_parts(matrix)
    return np.concatenate([high, low, high], axis=-1)


def right_blocks(matrix):
    high, low = two_parts(matrix)
    return np.concatenate([high, low, high], axis=-2)


@functools.cache
def tables():
    core = np.arange(2)[:, None, None, None]
    branch = np.arange(4)[None, :, None, None]
    freq = 8 * np.arange(RAD)[None, None, :, None] + core + 2 * branch
    row = np.arange(RAD)[None, None, None, :]
    angle = -2.0 * math.pi / 4096.0 * ((4 * freq + 1) * row % 4096)
    cos, sin = np.cos(angle), np.sin(angle)
    rows = np.concatenate([np.concatenate([cos, -sin], -1), np.concatenate([sin, cos], -1)], -2)
    scale = 1.0 / (LENGTH * math.sqrt(LENGTH))
    rows_back = np.swapaxes(rows, -1, -2) * scale
    column = np.arange(COLS)[None, None, None, :]
    angle = -2.0 * math.pi / (4 * LENGTH) * ((4 * freq + 1) * column % (4 * LENGTH))
    twiddle = np.stack([np.cos(angle), np.sin(angle)], axis=1).astype(np.float32)
    inner = np.arange(RAD)[None, :, None]
    outer = 4 * np.arange(RAD)[None, None, :] + np.arange(4)[:, None, None]
    angle = -2.0 * math.pi / COLS * (outer * inner % COLS)
    cos, sin = np.cos(angle), np.sin(angle)
    lanes = np.concatenate([np.concatenate([cos, sin], -1), np.concatenate([-sin, cos], -1)], -2)
    lanes_back = np.swapaxes(lanes, -1, -2)
    return (
        left_blocks(rows),
        left_blocks(rows_back),
        twiddle.reshape(2, 2, 4 * RAD, COLS),
        right_blocks(lanes),
        right_blocks(lanes_back),
    )


def split(value):
    high = value.astype(jnp.bfloat16)
    low = (value - high.astype(jnp.float32)).astype(jnp.bfloat16)
    return high, low


def butterfly(parts, sign):
    (ar, ai), (br, bi), (cr, ci), (dr, di) = parts
    pr, pi, mr, mi = ar + cr, ai + ci, ar - cr, ai - ci
    qr, qi, nr, ni = br + dr, bi + di, br - dr, bi - di
    first = (mr - sign * ni, mi + sign * nr)
    third = (mr + sign * ni, mi - sign * nr)
    return [(pr + qr, pi + qi), first, (pr - qr, pi - qi), third]


def turns(core):
    out = []
    for j in range(8):
        a = -2.0 * math.pi * j * 0.25 / 8.0
        b = -2.0 * math.pi * j * 1.25 / 8.0
        even = core == 0
        out.append(
            (
                jnp.where(even, jnp.float32(math.cos(a)), jnp.float32(math.cos(b))),
                jnp.where(even, jnp.float32(math.sin(a)), jnp.float32(math.sin(b))),
            )
        )
    return out


def dot(left, right):
    return lax.dot_general(left, right, (((1,), (0,)), ((), ())), preferred_element_type=jnp.float32)


def forward(core, x, rows, twiddle, lanes, work, spec):
    factors = turns(core)

    def columns(step, carry):
        cols = pl.ds(pl.multiple_of(step * WIDE, WIDE), WIDE)
        real = [x[4 * j : 4 * j + 4, :, :, cols].reshape(RAD, WIDE) for j in range(8)]
        parts = []
        for j in range(4):
            (ar, ai), (br, bi) = factors[j], factors[j + 4]
            parts.append((ar * real[j] + br * real[j + 4], ai * real[j] + bi * real[j + 4]))
        for branch, (re, im) in enumerate(butterfly(parts, -1.0)):
            high, low = split(jnp.concatenate([re, im], axis=0))
            out = dot(rows[branch], jnp.concatenate([high, high, low], axis=0))
            re, im = out[:RAD], out[RAD:]
            at = slice(branch * RAD, (branch + 1) * RAD)
            cos, sin = twiddle[0, at, cols], twiddle[1, at, cols]
            work[0, at, cols] = re * cos - im * sin
            work[1, at, cols] = re * sin + im * cos
        return carry

    lax.fori_loop(0, COLS // WIDE, columns, 0)

    def bands(step, carry):
        at = pl.ds(pl.multiple_of(step * RAD, RAD), RAD)
        parts = [(work[0, at, RAD * j : RAD * (j + 1)], work[1, at, RAD * j : RAD * (j + 1)]) for j in range(4)]
        for branch, (re, im) in enumerate(butterfly(parts, -1.0)):
            high, low = split(jnp.concatenate([re, im], axis=1))
            spec[branch, at, :] = dot(jnp.concatenate([high, high, low], axis=1), lanes[branch])
        return carry

    lax.fori_loop(0, 4, bands, 0)


def backward(core, left, right, rows_back, twiddle, lanes_back, wide, out):
    factors = turns(core)

    def bands(step, carry):
        at = pl.ds(pl.multiple_of(step * RAD, RAD), RAD)
        parts = []
        for branch in range(4):
            lr, li = left[branch, at, :RAD], left[branch, at, RAD:]
            rr, ri = right[branch, at, :RAD], right[branch, at, RAD:]
            high, low = split(jnp.concatenate([lr * rr + li * ri, li * rr - lr * ri], axis=1))
            back = dot(jnp.concatenate([high, high, low], axis=1), lanes_back[branch])
            parts.append((back[:, :RAD], back[:, RAD:]))
        for j, (re, im) in enumerate(butterfly(parts, 1.0)):
            cols = slice(RAD * j, RAD * (j + 1))
            cos, sin = twiddle[0, at, cols], twiddle[1, at, cols]
            high, low = split(jnp.concatenate([re * cos + im * sin, im * cos - re * sin], axis=0))
            wide[step, 0, :, cols] = high
            wide[step, 1, :, cols] = low
        return carry

    lax.fori_loop(0, 4, bands, 0)

    def columns(step, carry):
        cols = pl.ds(pl.multiple_of(step * WIDE, WIDE), WIDE)
        parts = []
        for branch in range(4):
            high, low = wide[branch, 0, :, cols], wide[branch, 1, :, cols]
            back = dot(rows_back[branch], jnp.concatenate([high, high, low], axis=0))
            parts.append((back[:RAD], back[RAD:]))
        sums = butterfly(parts, 1.0)
        for j in range(8):
            re, im = sums[j % 4]
            value = factors[j][0] * re + factors[j][1] * im
            out[4 * j : 4 * j + 4, :, :, cols] = value.reshape(4, 2, ROWS, WIDE)
        return carry

    lax.fori_loop(0, COLS // WIDE, columns, 0)


def kernel(
    grad, inputs, filters, rows_all, rows_back_all, twiddle_all, lanes_all, lanes_back_all,
    grad_out, filter_out,
    x, spec, work, wide, part, near, total, far, rows, rows_back, twiddle, lanes, lanes_back,
    table_sem, own_sem, send_sem, recv_sem, pass_send, pass_recv, part_send, part_recv,
    far_send, far_recv, out_send, out_recv, out_own,
):
    me, group = lax.axis_index("seq"), lax.axis_index("dp")
    core, chip = lax.rem(me, 2), me // 2
    side = lax.rem(chip // 4, 2)
    sibling = {"seq": chip * 2 + 1 - core}
    partner = {"dp": 1 - group}
    signals = (grad, inputs, filters)

    def remote(src, dst, send, recv, device):
        return pltpu.make_async_remote_copy(
            src_ref=src, dst_ref=dst, send_sem=send, recv_sem=recv, device_id=device, device_id_type=MESH
        )

    loads = [
        pltpu.make_async_copy(rows_all.at[core], rows, table_sem.at[0]),
        pltpu.make_async_copy(rows_back_all.at[core], rows_back, table_sem.at[1]),
        pltpu.make_async_copy(twiddle_all.at[core], twiddle, table_sem.at[2]),
        pltpu.make_async_copy(lanes_all, lanes, table_sem.at[3]),
        pltpu.make_async_copy(lanes_back_all, lanes_back, table_sem.at[4]),
    ]
    for load in loads:
        load.start()
    owns = [pltpu.make_async_copy(signals[q].at[chip], x.at[q, chip, core], own_sem.at[q]) for q in range(3)]
    for own in owns:
        own.start()

    barrier = pltpu.get_barrier_semaphore()

    def greet(step, carry):
        other = jnp.bitwise_xor(chip, step) * 2 + core
        pl.semaphore_signal(barrier, inc=1, device_id={"seq": other}, device_id_type=MESH)
        return carry

    def greet_far(step, carry):
        other = jnp.bitwise_xor(chip, step) * 2 + core
        pl.semaphore_signal(barrier, inc=1, device_id={"dp": 1 - group, "seq": other}, device_id_type=MESH)
        return carry

    lax.fori_loop(1, CHIPS, greet, 0)
    lax.fori_loop(0, CHIPS, greet_far, 0)
    pl.semaphore_signal(barrier, inc=1, device_id=sibling, device_id_type=MESH)
    pl.semaphore_wait(barrier, 2 * CHIPS)

    for q in range(3):

        def scatter(step, carry, q=q):
            other = jnp.bitwise_xor(chip, step)
            remote(
                signals[q].at[other], x.at[q, chip, core], send_sem.at[q], recv_sem.at[q], {"seq": other * 2 + core}
            ).start()
            return carry

        lax.fori_loop(1, CHIPS, scatter, 0)

    def all_but_own(q, sem):
        ref = x.at[q, pl.ds(0, CHIPS - 1), 0]
        return pltpu.make_async_copy(ref, ref, sem)

    def passing(q):
        half = x.at[q, :, core]
        return remote(half, half, pass_send.at[q], pass_recv.at[q], sibling)

    def arrive(q):
        owns[q].wait()
        all_but_own(q, recv_sem.at[q]).wait()
        passing(q).start()

    def exchange(k):
        return remote(part.at[k, :, 1 - core], near.at[k], part_send.at[k], part_recv.at[k], sibling)

    def reduce(k):
        exchange(k).wait_recv()
        for j in range(8):
            total[k, j // 2, j % 2] = part[k, 4 * j : 4 * j + 4, core] + near[k, 4 * j : 4 * j + 4]

    far_copy = remote(total.at[1, :, 1 - group], far, far_send, far_recv, partner)

    arrive(0)
    for load in loads:
        load.wait()
    passing(0).wait_recv()
    forward(core, x.at[0], rows, twiddle, lanes, work, spec.at[0])
    arrive(1)
    passing(1).wait_recv()
    forward(core, x.at[1], rows, twiddle, lanes, work, spec.at[1])
    backward(core, spec.at[0], spec.at[1], rows_back, twiddle, lanes_back, wide, part.at[1])
    exchange(1).start()
    reduce(1)
    far_copy.start()
    arrive(2)
    far_copy.wait_recv()
    for j in range(4):
        total[1, j, group] = total[1, j, group] + far[j]

    def filter_block(step):
        other = (step // 4) * 8 + group * 4 + lax.rem(step, 4)
        return other, total.at[1, step // 4, group, lax.rem(step, 4)]

    def filter_near(step, carry):
        other, block = filter_block(step)

        @pl.when(other != chip)
        def _():
            remote(block, filter_out.at[chip], out_send.at[1], out_recv.at[1], {"seq": other * 2 + core}).start()

        @pl.when(other == chip)
        def _():
            pltpu.make_async_copy(block, filter_out.at[chip], out_own.at[1]).start()

        return carry

    def filter_far(step, carry):
        other, block = filter_block(step)
        remote(
            block, filter_out.at[chip], out_send.at[2], out_recv.at[1], {"dp": 1 - group, "seq": other * 2 + core}
        ).start()
        return carry

    lax.fori_loop(0, CHIPS // 2, filter_near, 0)
    lax.fori_loop(0, CHIPS // 2, filter_far, 0)
    passing(2).wait_recv()
    forward(core, x.at[2], rows, twiddle, lanes, work, spec.at[2])
    backward(core, spec.at[0], spec.at[2], rows_back, twiddle, lanes_back, wide, part.at[0])
    exchange(0).start()
    reduce(0)

    def gradient(step, carry):
        other = jnp.bitwise_xor(chip, step)
        block = total.at[0, other // 8, lax.rem(other // 4, 2), lax.rem(other, 4)]
        remote(block, grad_out.at[chip], out_send.at[0], out_recv.at[0], {"seq": other * 2 + core}).start()
        return carry

    lax.fori_loop(1, CHIPS, gradient, 0)
    mine = total.at[0, chip // 8, side, lax.rem(chip, 4)]
    own_grad = pltpu.make_async_copy(mine, grad_out.at[chip], out_own.at[0])
    own_grad.start()

    def wait_blocks(count, sem):
        ref = x.at[0, pl.ds(0, count), 0]
        pltpu.make_async_copy(ref, ref, sem).wait()

    for q in range(3):
        all_but_own(q, send_sem.at[q]).wait()
        passing(q).wait_send()
    for k in range(2):
        exchange(k).wait_send()
    far_copy.wait_send()
    own_grad.wait()
    wait_blocks(CHIPS - 1, out_send.at[0])
    wait_blocks(CHIPS // 2, out_send.at[2])

    @pl.when(side == group)
    def _():
        wait_blocks(CHIPS // 2 - 1, out_send.at[1])
        wait_blocks(CHIPS - 1, out_recv.at[1])
        pltpu.make_async_copy(mine, filter_out.at[chip], out_own.at[1]).wait()

    @pl.when(side != group)
    def _():
        wait_blocks(CHIPS // 2, out_send.at[1])
        wait_blocks(CHIPS, out_recv.at[1])

    wait_blocks(CHIPS - 1, out_recv.at[0])


def shards(inputs, grad_out, filters, skip):
    channels = filters.shape[0]
    length = filters.shape[1]
    shape = (channels, ROWS, COLS)
    constants = tables()
    vmem, dma = pltpu.VMEM, pltpu.SemaphoreType.DMA
    any_space = pl.BlockSpec(memory_space=pl.ANY)
    conv, filter_grad = pl.pallas_call(
        kernel,
        out_shape=[jax.ShapeDtypeStruct(shape, jnp.float32)] * 2,
        in_specs=[any_space] * 8,
        out_specs=[pl.BlockSpec(memory_space=pltpu.VMEM)] * 2,
        scratch_shapes=[
            vmem((3, CHIPS, 2, ROWS, COLS), jnp.float32),
            vmem((3, 4, 4 * RAD, 2 * RAD), jnp.float32),
            vmem((2, 4 * RAD, COLS), jnp.float32),
            vmem((4, 2, 2 * RAD, COLS), jnp.bfloat16),
            vmem((2, CHIPS, 2, ROWS, COLS), jnp.float32),
            vmem((2, CHIPS, ROWS, COLS), jnp.float32),
            vmem((2, 4, 2, 4, ROWS, COLS), jnp.float32),
            vmem((4, 4, ROWS, COLS), jnp.float32),
            vmem(constants[0].shape[1:], jnp.bfloat16),
            vmem(constants[1].shape[1:], jnp.bfloat16),
            vmem(constants[2].shape[1:], jnp.float32),
            vmem(constants[3].shape, jnp.bfloat16),
            vmem(constants[4].shape, jnp.bfloat16),
            dma((5,)), dma((3,)), dma((3,)), dma((3,)), dma((3,)), dma((3,)), dma((2,)), dma((2,)),
            dma(()), dma(()), dma((3,)), dma((2,)), dma((2,)),
        ],
        compiler_params=pltpu.CompilerParams(
            collective_id=0, has_side_effects=True, vmem_limit_bytes=56 * 2**20
        ),
        cost_estimate=pl.CostEstimate(flops=9 * 10**9, bytes_accessed=2 * 10**7, transcendentals=0),
    )(
        grad_out.reshape(shape), inputs.reshape(shape), filters.reshape(shape),
        *(jnp.asarray(table) for table in constants),
    )
    grad_in = conv.reshape(1, channels, length) + skip[None, :, None] * grad_out
    return (grad_in, filter_grad.reshape(channels, length))


def solution(mesh):
    return jax.shard_map(
        shards,
        mesh=mesh,
        in_specs=(P("dp", None, "seq"), P("dp", None, "seq"), P(None, "seq"), P()),
        out_specs=(P("dp", None, "seq"), P(None, "seq")),
        check_vma=False,
    )
```

```python
import functools
import math

import jax
import jax.numpy as jnp
import ml_dtypes
import numpy as np
from jax import lax
from jax.experimental import pallas as pl
from jax.experimental.pallas import tpu as pltpu
from jax.sharding import PartitionSpec as P

MESH = pl.DeviceIdType.MESH
CHIPS = 32
ROWS = 16
COLS = 512
RAD = 128
LENGTH = CHIPS * 2 * ROWS * COLS
WIDE = 256


def two_parts(matrix):
    high = matrix.astype(ml_dtypes.bfloat16)
    low = (matrix - high.astype(np.float64)).astype(ml_dtypes.bfloat16)
    return high, low


def left_blocks(matrix):
    high, low = two_parts(matrix)
    return np.concatenate([high, low, high], axis=-1)


def right_blocks(matrix):
    high, low = two_parts(matrix)
    return np.concatenate([high, low, high], axis=-2)


@functools.cache
def tables():
    core = np.arange(2)[:, None, None, None]
    branch = np.arange(4)[None, :, None, None]
    freq = 8 * np.arange(RAD)[None, None, :, None] + core + 2 * branch
    row = np.arange(RAD)[None, None, None, :]
    angle = -2.0 * math.pi / 4096.0 * ((4 * freq + 1) * row % 4096)
    cos, sin = np.cos(angle), np.sin(angle)
    rows = np.concatenate([np.concatenate([cos, -sin], -1), np.concatenate([sin, cos], -1)], -2)
    scale = 1.0 / (LENGTH * math.sqrt(LENGTH))
    rows_back = np.swapaxes(rows, -1, -2) * scale
    column = np.arange(COLS)[None, None, None, :]
    angle = -2.0 * math.pi / (4 * LENGTH) * ((4 * freq + 1) * column % (4 * LENGTH))
    twiddle = np.stack([np.cos(angle), np.sin(angle)], axis=1).astype(np.float32)
    inner = np.arange(RAD)[None, :, None]
    outer = 4 * np.arange(RAD)[None, None, :] + np.arange(4)[:, None, None]
    angle = -2.0 * math.pi / COLS * (outer * inner % COLS)
    cos, sin = np.cos(angle), np.sin(angle)
    lanes = np.concatenate([np.concatenate([cos, sin], -1), np.concatenate([-sin, cos], -1)], -2)
    lanes_back = np.swapaxes(lanes, -1, -2)
    return (
        left_blocks(rows),
        left_blocks(rows_back),
        twiddle.reshape(2, 2, 4 * RAD, COLS),
        right_blocks(lanes),
        right_blocks(lanes_back),
    )


def split(value):
    high = value.astype(jnp.bfloat16)
    low = (value - high.astype(jnp.float32)).astype(jnp.bfloat16)
    return high, low


def butterfly(parts, sign):
    (ar, ai), (br, bi), (cr, ci), (dr, di) = parts
    pr, pi, mr, mi = ar + cr, ai + ci, ar - cr, ai - ci
    qr, qi, nr, ni = br + dr, bi + di, br - dr, bi - di
    first = (mr - sign * ni, mi + sign * nr)
    third = (mr + sign * ni, mi - sign * nr)
    return [(pr + qr, pi + qi), first, (pr - qr, pi - qi), third]


def turns(core):
    out = []
    for j in range(8):
        a = -2.0 * math.pi * j * 0.25 / 8.0
        b = -2.0 * math.pi * j * 1.25 / 8.0
        even = core == 0
        out.append(
            (
                jnp.where(even, jnp.float32(math.cos(a)), jnp.float32(math.cos(b))),
                jnp.where(even, jnp.float32(math.sin(a)), jnp.float32(math.sin(b))),
            )
        )
    return out


def dot(left, right):
    return lax.dot_general(left, right, (((1,), (0,)), ((), ())), preferred_element_type=jnp.float32)


def forward(core, x, rows, twiddle, lanes, work, spec):
    factors = turns(core)

    def columns(step, carry):
        cols = pl.ds(pl.multiple_of(step * WIDE, WIDE), WIDE)
        real = [x[4 * j : 4 * j + 4, :, :, cols].reshape(RAD, WIDE) for j in range(8)]
        parts = []
        for j in range(4):
            (ar, ai), (br, bi) = factors[j], factors[j + 4]
            parts.append((ar * real[j] + br * real[j + 4], ai * real[j] + bi * real[j + 4]))
        for branch, (re, im) in enumerate(butterfly(parts, -1.0)):
            high, low = split(jnp.concatenate([re, im], axis=0))
            out = dot(rows[branch], jnp.concatenate([high, high, low], axis=0))
            re, im = out[:RAD], out[RAD:]
            at = slice(branch * RAD, (branch + 1) * RAD)
            cos, sin = twiddle[0, at, cols], twiddle[1, at, cols]
            work[0, at, cols] = re * cos - im * sin
            work[1, at, cols] = re * sin + im * cos
        return carry

    lax.fori_loop(0, COLS // WIDE, columns, 0)

    def bands(step, carry):
        at = pl.ds(pl.multiple_of(step * RAD, RAD), RAD)
        parts = [(work[0, at, RAD * j : RAD * (j + 1)], work[1, at, RAD * j : RAD * (j + 1)]) for j in range(4)]
        for branch, (re, im) in enumerate(butterfly(parts, -1.0)):
            high, low = split(jnp.concatenate([re, im], axis=1))
            spec[branch, at, :] = dot(jnp.concatenate([high, high, low], axis=1), lanes[branch])
        return carry

    lax.fori_loop(0, 4, bands, 0)


def backward(core, left, right, rows_back, twiddle, lanes_back, wide, out):
    factors = turns(core)

    def bands(step, carry):
        at = pl.ds(pl.multiple_of(step * RAD, RAD), RAD)
        parts = []
        for branch in range(4):
            lr, li = left[branch, at, :RAD], left[branch, at, RAD:]
            rr, ri = right[branch, at, :RAD], right[branch, at, RAD:]
            high, low = split(jnp.concatenate([lr * rr + li * ri, li * rr - lr * ri], axis=1))
            back = dot(jnp.concatenate([high, high, low], axis=1), lanes_back[branch])
            parts.append((back[:, :RAD], back[:, RAD:]))
        for j, (re, im) in enumerate(butterfly(parts, 1.0)):
            cols = slice(RAD * j, RAD * (j + 1))
            cos, sin = twiddle[0, at, cols], twiddle[1, at, cols]
            high, low = split(jnp.concatenate([re * cos + im * sin, im * cos - re * sin], axis=0))
            wide[step, 0, :, cols] = high
            wide[step, 1, :, cols] = low
        return carry

    lax.fori_loop(0, 4, bands, 0)

    def columns(step, carry):
        cols = pl.ds(pl.multiple_of(step * WIDE, WIDE), WIDE)
        parts = []
        for branch in range(4):
            high, low = wide[branch, 0, :, cols], wide[branch, 1, :, cols]
            back = dot(rows_back[branch], jnp.concatenate([high, high, low], axis=0))
            parts.append((back[:RAD], back[RAD:]))
        sums = butterfly(parts, 1.0)
        for j in range(8):
            re, im = sums[j % 4]
            value = factors[j][0] * re + factors[j][1] * im
            out[4 * j : 4 * j + 4, :, :, cols] = value.reshape(4, 2, ROWS, WIDE)
        return carry

    lax.fori_loop(0, COLS // WIDE, columns, 0)


def kernel(
    grad, filters, inputs, rows_all, rows_back_all, twiddle_all, lanes_all, lanes_back_all,
    landed,
    raw, rolled, x, spec, work, wide, part, near, total, far, rows, rows_back, twiddle, lanes, lanes_back,
    table_sem, raw_sem, own_sem, send_sem, recv_sem, pass_send, pass_recv, part_send, part_recv,
    far_send, far_recv, out_send, out_recv, out_own,
):
    me, group = lax.axis_index("seq"), lax.axis_index("dp")
    core, chip = lax.rem(me, 2), me // 2
    side = lax.rem(chip // 8 + chip, 2)
    flip = 4 * group
    channel = jnp.bitwise_xor(chip, flip)
    sibling = {"seq": chip * 2 + 1 - core}
    partner = {"dp": 1 - group, "seq": jnp.bitwise_xor(chip, 4) * 2 + core}
    signals = (grad, filters, inputs)

    def remote(src, dst, send, recv, device):
        return pltpu.make_async_remote_copy(
            src_ref=src, dst_ref=dst, send_sem=send, recv_sem=recv, device_id=device, device_id_type=MESH
        )

    raws = [pltpu.make_async_copy(signals[q], raw.at[q], raw_sem.at[q]) for q in range(3)]
    for copy in raws:
        copy.start()
    loads = [
        pltpu.make_async_copy(rows_all.at[core], rows, table_sem.at[0]),
        pltpu.make_async_copy(twiddle_all.at[core], twiddle, table_sem.at[1]),
        pltpu.make_async_copy(lanes_all, lanes, table_sem.at[2]),
        pltpu.make_async_copy(lanes_back_all, lanes_back, table_sem.at[3]),
        pltpu.make_async_copy(rows_back_all.at[core], rows_back, table_sem.at[4]),
    ]
    for load in loads:
        load.start()

    barrier = pltpu.get_barrier_semaphore()

    def greet(step, carry):
        other = jnp.bitwise_xor(chip, step) * 2 + core
        pl.semaphore_signal(barrier, inc=1, device_id={"seq": other}, device_id_type=MESH)
        return carry

    lax.fori_loop(1, CHIPS, greet, 0)
    for other in (sibling, partner):
        pl.semaphore_signal(barrier, inc=1, device_id=other, device_id_type=MESH)

    def roll(q):
        raws[q].wait()
        for n in range(ROWS):
            rolled[q, :, n, :] = raw[q, :, n * COLS : (n + 1) * COLS]

    def own(q):
        return pltpu.make_async_copy(rolled.at[q, channel], x.at[q, chip, core], own_sem.at[q])

    def scatter(q):
        def one(step, carry):
            other = jnp.bitwise_xor(chip, step)
            block = rolled.at[q, jnp.bitwise_xor(other, flip)]
            remote(block, x.at[q, chip, core], send_sem.at[q], recv_sem.at[q], {"seq": other * 2 + core}).start()
            return carry

        lax.fori_loop(1, CHIPS, one, 0)
        own(q).start()

    def all_but_own(q, sem):
        ref = x.at[q, pl.ds(0, CHIPS - 1), 0]
        return pltpu.make_async_copy(ref, ref, sem)

    def passing(q):
        half = x.at[q, :, core]
        return remote(half, half, pass_send.at[q], pass_recv.at[q], sibling)

    def arrive(q):
        own(q).wait()
        all_but_own(q, recv_sem.at[q]).wait()
        passing(q).start()

    def exchange(k):
        return remote(part.at[k, :, 1 - core], near.at[k], part_send.at[k], part_recv.at[k], sibling)

    def reduce(k):
        exchange(k).wait_recv()
        for j in range(8):
            total[k, j // 2, j % 2] = part[k, 4 * j : 4 * j + 4, core] + near[k, 4 * j : 4 * j + 4]

    def place(owner, piece, i):
        diagonal = owner + 2 * lax.rem(piece // 2 + channel // 8, 2)
        return i, lax.rem(piece + channel // 4, 2), lax.rem(diagonal + 4 - i, 4)

    def far_start(piece):
        for i in range(4):
            at = place(1 - group, piece, i)
            remote(
                total.at[1, at[0], at[1], at[2]], far.at[piece, i], far_send.at[piece], far_recv.at[piece], partner
            ).start()

    def far_wait(piece, sem):
        ref = far.at[piece]
        pltpu.make_async_copy(ref, ref, sem.at[piece]).wait()

    roll(0)
    pl.semaphore_wait(barrier, CHIPS + 1)
    scatter(0)
    roll(1)
    roll(2)
    all_but_own(0, send_sem.at[0]).wait()
    scatter(1)
    arrive(0)
    for load in loads:
        load.wait()
    passing(0).wait_recv()
    forward(core, x.at[0], rows, twiddle, lanes, work, spec.at[0])
    all_but_own(1, send_sem.at[1]).wait()
    scatter(2)
    arrive(1)
    passing(1).wait_recv()
    forward(core, x.at[1], rows, twiddle, lanes, work, spec.at[1])
    backward(core, spec.at[0], spec.at[1], rows_back, twiddle, lanes_back, wide, part.at[0])
    exchange(0).start()
    reduce(0)

    def gradient(step, carry):
        other = jnp.bitwise_xor(chip, step)
        block = total.at[0, other // 8, lax.rem(other // 4, 2), lax.rem(other, 4)]
        remote(block, landed.at[0, channel], out_send.at[0], out_recv.at[0], {"seq": other * 2 + core}).start()
        return carry

    all_but_own(2, send_sem.at[2]).wait()
    lax.fori_loop(1, CHIPS, gradient, 0)
    mine = [total.at[k, chip // 8, lax.rem(chip // 4, 2), lax.rem(chip, 4)] for k in range(2)]
    own_grad = pltpu.make_async_copy(mine[0], landed.at[0, channel], out_own.at[0])
    own_grad.start()

    arrive(2)
    passing(2).wait_recv()
    forward(core, x.at[2], rows, twiddle, lanes, work, spec.at[2])
    backward(core, spec.at[0], spec.at[2], rows_back, twiddle, lanes_back, wide, part.at[1])
    exchange(1).start()
    reduce(1)
    for piece in range(4):
        far_start(piece)
    for piece in range(4):
        far_wait(piece, far_recv)

        def settle(i, carry, piece=piece):
            at = place(group, piece, i)
            block = total.at[1, at[0], at[1], at[2]]
            block[...] = block[...] + far[piece, i]
            other = at[0] * 8 + at[1] * 4 + at[2]

            @pl.when(other != chip)
            def _():
                remote(block, landed.at[1, channel], out_send.at[1], out_recv.at[1], {"seq": other * 2 + core}).start()

            @pl.when(other == chip)
            def _():
                pltpu.make_async_copy(block, landed.at[1, channel], out_own.at[1]).start()

            device = {"dp": 1 - group, "seq": other * 2 + core}
            remote(block, landed.at[1, channel], out_send.at[2], out_recv.at[1], device).start()
            return carry

        lax.fori_loop(0, 4, settle, 0)

    def wait_blocks(count, sem):
        ref = x.at[0, pl.ds(0, count), 0]
        pltpu.make_async_copy(ref, ref, sem).wait()

    for q in range(3):
        passing(q).wait_send()
    for k in range(2):
        exchange(k).wait_send()
    for piece in range(4):
        far_wait(piece, far_send)

    @pl.when(side == group)
    def _():
        wait_blocks(CHIPS // 2 - 1, out_send.at[1])
        wait_blocks(CHIPS - 1, out_recv.at[1])
        pltpu.make_async_copy(mine[1], landed.at[1, channel], out_own.at[1]).wait()

    @pl.when(side != group)
    def _():
        wait_blocks(CHIPS // 2, out_send.at[1])
        wait_blocks(CHIPS, out_recv.at[1])

    wait_blocks(CHIPS // 2, out_send.at[2])
    wait_blocks(CHIPS - 1, out_send.at[0])
    own_grad.wait()
    wait_blocks(CHIPS - 1, out_recv.at[0])


def finish(landed, grad, skip, grad_in, filter_grad):
    channels = grad.shape[0]
    shape = (channels, skip.shape[1])
    chosen = lax.broadcasted_iota(jnp.int32, shape, 1) == (
        lax.broadcasted_iota(jnp.int32, shape, 0) + pl.program_id(0) * channels
    )
    gain = jnp.sum(jnp.where(chosen, skip[...], 0.0), axis=1, keepdims=True)
    for n in range(ROWS):
        at = slice(n * COLS, (n + 1) * COLS)
        grad_in[:, at] = landed[0, :, n, :] + gain * grad[:, at]
        filter_grad[:, at] = landed[1, :, n, :]


def shards(inputs, grad_out, filters, skip):
    channels, length = filters.shape
    constants = tables()
    vmem, dma = pltpu.VMEM, pltpu.SemaphoreType.DMA
    any_space = pl.BlockSpec(memory_space=pl.ANY)
    grad = grad_out.reshape(channels, length)
    landed = pl.pallas_call(
        kernel,
        out_shape=jax.ShapeDtypeStruct((2, CHIPS, ROWS, COLS), jnp.float32),
        in_specs=[any_space] * 8,
        out_specs=any_space,
        scratch_shapes=[
            vmem((3, channels, length), jnp.float32),
            vmem((3, CHIPS, ROWS, COLS), jnp.float32),
            vmem((3, CHIPS, 2, ROWS, COLS), jnp.float32),
            vmem((3, 4, 4 * RAD, 2 * RAD), jnp.float32),
            vmem((2, 4 * RAD, COLS), jnp.float32),
            vmem((4, 2, 2 * RAD, COLS), jnp.bfloat16),
            vmem((2, CHIPS, 2, ROWS, COLS), jnp.float32),
            vmem((2, CHIPS, ROWS, COLS), jnp.float32),
            vmem((2, 4, 2, 4, ROWS, COLS), jnp.float32),
            vmem((4, 4, ROWS, COLS), jnp.float32),
            vmem(constants[0].shape[1:], jnp.bfloat16),
            vmem(constants[1].shape[1:], jnp.bfloat16),
            vmem(constants[2].shape[1:], jnp.float32),
            vmem(constants[3].shape, jnp.bfloat16),
            vmem(constants[4].shape, jnp.bfloat16),
            dma((5,)), dma((3,)), dma((3,)), dma((3,)), dma((3,)), dma((3,)), dma((3,)), dma((2,)), dma((2,)),
            dma((4,)), dma((4,)), dma((3,)), dma((2,)), dma((2,)),
        ],
        compiler_params=pltpu.CompilerParams(
            collective_id=0, has_side_effects=True, vmem_limit_bytes=56 * 2**20
        ),
        cost_estimate=pl.CostEstimate(flops=9 * 10**9, bytes_accessed=2 * 10**7, transcendentals=0),
    )(
        grad, filters, inputs.reshape(channels, length),
        *(jnp.asarray(table) for table in constants),
    )
    flat = pl.BlockSpec((8, length), lambda i: (i, 0))
    grad_in, filter_grad = pl.pallas_call(
        finish,
        out_shape=[jax.ShapeDtypeStruct((channels, length), jnp.float32)] * 2,
        grid=(channels // 8,),
        in_specs=[
            pl.BlockSpec((2, 8, ROWS, COLS), lambda i: (0, i, 0, 0)),
            flat,
            pl.BlockSpec((1, channels), lambda i: (0, 0)),
        ],
        out_specs=[flat, flat],
        cost_estimate=pl.CostEstimate(flops=10**6, bytes_accessed=5 * 2**20, transcendentals=0),
    )(landed, grad, skip.reshape(1, channels))
    return (grad_in.reshape(1, channels, length), filter_grad)


def solution(mesh):
    return jax.shard_map(
        shards,
        mesh=mesh,
        in_specs=(P("dp", None, "seq"), P("dp", None, "seq"), P(None, "seq"), P()),
        out_specs=(P("dp", None, "seq"), P(None, "seq")),
        check_vma=False,
    )
```

```python
import functools
import math

import jax
import jax.numpy as jnp
import ml_dtypes
import numpy as np
from jax import lax
from jax.experimental import pallas as pl
from jax.experimental.pallas import tpu as pltpu
from jax.sharding import PartitionSpec as P

MESH = pl.DeviceIdType.MESH
CHIPS = 32
ROWS = 16
COLS = 512
RAD = 128
LENGTH = CHIPS * 2 * ROWS * COLS


def two_parts(matrix):
    high = matrix.astype(ml_dtypes.bfloat16)
    low = (matrix - high.astype(np.float64)).astype(ml_dtypes.bfloat16)
    return high, low


def left_blocks(matrix):
    high, low = two_parts(matrix)
    return np.concatenate([high, low, high], axis=-1)


def right_blocks(matrix):
    high, low = two_parts(matrix)
    return np.concatenate([high, low, high], axis=-2)


@functools.cache
def tables():
    core = np.arange(2)[:, None, None, None]
    branch = np.arange(4)[None, :, None, None]
    freq = 8 * np.arange(RAD)[None, None, :, None] + core + 2 * branch
    row = np.arange(RAD)[None, None, None, :]
    angle = -2.0 * math.pi / 4096.0 * ((4 * freq + 1) * row % 4096)
    cos, sin = np.cos(angle), np.sin(angle)
    rows = np.concatenate([np.concatenate([cos, -sin], -1), np.concatenate([sin, cos], -1)], -2)
    scale = 1.0 / (LENGTH * math.sqrt(LENGTH))
    rows_back = np.swapaxes(rows, -1, -2) * scale
    column = np.arange(COLS)[None, None, None, :]
    angle = -2.0 * math.pi / (4 * LENGTH) * ((4 * freq + 1) * column % (4 * LENGTH))
    twiddle = np.stack([np.cos(angle), np.sin(angle)], axis=1).astype(np.float32)
    inner = np.arange(RAD)[None, :, None]
    outer = 4 * np.arange(RAD)[None, None, :] + np.arange(4)[:, None, None]
    angle = -2.0 * math.pi / COLS * (outer * inner % COLS)
    cos, sin = np.cos(angle), np.sin(angle)
    lanes = np.concatenate([np.concatenate([cos, sin], -1), np.concatenate([-sin, cos], -1)], -2)
    lanes_back = np.swapaxes(lanes, -1, -2)
    return (
        left_blocks(rows),
        left_blocks(rows_back),
        twiddle.reshape(2, 2, 4 * RAD, COLS),
        right_blocks(lanes),
        right_blocks(lanes_back),
    )


def split(value):
    high = value.astype(jnp.bfloat16)
    low = (value - high.astype(jnp.float32)).astype(jnp.bfloat16)
    return high, low


def butterfly(parts, sign):
    (ar, ai), (br, bi), (cr, ci), (dr, di) = parts
    pr, pi, mr, mi = ar + cr, ai + ci, ar - cr, ai - ci
    qr, qi, nr, ni = br + dr, bi + di, br - dr, bi - di
    first = (mr - sign * ni, mi + sign * nr)
    third = (mr + sign * ni, mi - sign * nr)
    return [(pr + qr, pi + qi), first, (pr - qr, pi - qi), third]


def turns(half):
    angles = [-2.0 * math.pi * j * (half + 0.25) / 8.0 for j in range(8)]
    return [(math.cos(angle), math.sin(angle)) for angle in angles]


def dot(left, right):
    return lax.dot_general(left, right, (((1,), (0,)), ((), ())), preferred_element_type=jnp.float32)


def forward(x, rows, twiddle, lanes, work, spec):
    real = [x[4 * j : 4 * j + 4].reshape(RAD, COLS) for j in range(8)]
    for half in range(2):
        factors = turns(half)
        parts = []
        for j in range(4):
            (ar, ai), (br, bi) = factors[j], factors[j + 4]
            parts.append((ar * real[j] + br * real[j + 4], ai * real[j] + bi * real[j + 4]))
        for branch, (re, im) in enumerate(butterfly(parts, -1.0)):
            high, low = split(jnp.concatenate([re, im], axis=0))
            out = dot(rows[half, branch], jnp.concatenate([high, high, low], axis=0))
            re, im = out[:RAD], out[RAD:]
            at = slice(branch * RAD, (branch + 1) * RAD)
            cos, sin = twiddle[half, 0, at], twiddle[half, 1, at]
            work[half, 0, at] = re * cos - im * sin
            work[half, 1, at] = re * sin + im * cos

    def bands(half, carry):
        parts = [
            (work[half, 0, :, RAD * j : RAD * (j + 1)], work[half, 1, :, RAD * j : RAD * (j + 1)]) for j in range(4)
        ]
        for branch, (re, im) in enumerate(butterfly(parts, -1.0)):
            high, low = split(jnp.concatenate([re, im], axis=1))
            spec[half, branch] = dot(jnp.concatenate([high, high, low], axis=1), lanes[branch])
        return carry

    lax.fori_loop(0, 2, bands, 0)


def backward(left, right, rows_back, twiddle, lanes_back, wide, out):
    def bands(half, carry):
        parts = []
        for branch in range(4):
            lr, li = left[half, branch, :, :RAD], left[half, branch, :, RAD:]
            rr, ri = right[half, branch, :, :RAD], right[half, branch, :, RAD:]
            high, low = split(jnp.concatenate([lr * rr + li * ri, li * rr - lr * ri], axis=1))
            back = dot(jnp.concatenate([high, high, low], axis=1), lanes_back[branch])
            parts.append((back[:, :RAD], back[:, RAD:]))
        for j, (re, im) in enumerate(butterfly(parts, 1.0)):
            cols = slice(RAD * j, RAD * (j + 1))
            cos, sin = twiddle[half, 0, :, cols], twiddle[half, 1, :, cols]
            for side, value in enumerate((re * cos + im * sin, im * cos - re * sin)):
                high, low = split(value.reshape(4, RAD, RAD))
                wide[half, :, 0, side * RAD : (side + 1) * RAD, cols] = high
                wide[half, :, 1, side * RAD : (side + 1) * RAD, cols] = low
        return carry

    lax.fori_loop(0, 2, bands, 0)
    values = [0.0] * 8
    for half in range(2):
        factors = turns(half)
        parts = []
        for branch in range(4):
            high, low = wide[half, branch, 0], wide[half, branch, 1]
            back = dot(rows_back[half, branch], jnp.concatenate([high, high, low], axis=0))
            parts.append((back[:RAD], back[RAD:]))
        sums = butterfly(parts, 1.0)
        for j in range(8):
            re, im = sums[j % 4]
            values[j] = values[j] + (factors[j][0] * re + factors[j][1] * im)
    for j in range(8):
        out[4 * j : 4 * j + 4] = values[j].reshape(4, 2, ROWS, COLS)


def kernel(
    grad, inputs, filters, rows_all, rows_back_all, twiddle_all, lanes_all, lanes_back_all,
    landed,
    raw, rolled, x, spec, work, wide, part, far, rows, rows_back, twiddle, lanes, lanes_back,
    table_sem, raw_sem, own_sem, send_sem, recv_sem, pass_send, pass_recv, ready, far_send, far_recv,
    out_send, out_recv, out_own,
):
    me, group = lax.axis_index("seq"), lax.axis_index("dp")
    core, chip = lax.rem(me, 2), me // 2
    side = lax.rem(chip // 8 + chip, 2)
    flip = 4 * group
    channel = jnp.bitwise_xor(chip, flip)
    sibling = {"seq": chip * 2 + 1 - core}
    partner = {"dp": 1 - group, "seq": jnp.bitwise_xor(chip, 4) * 2 + core}
    signals = (grad, inputs, filters)
    bulk = rolled.reshape(3 * CHIPS, ROWS, COLS)
    goals = (core, 1, 0)

    def remote(src, dst, send, recv, device):
        return pltpu.make_async_remote_copy(
            src_ref=src, dst_ref=dst, send_sem=send, recv_sem=recv, device_id=device, device_id_type=MESH
        )

    raws = [pltpu.make_async_copy(signals[q], raw.at[q], raw_sem.at[q]) for q in range(3)]
    for copy in raws:
        copy.start()
    loads = [
        pltpu.make_async_copy(rows_all, rows, table_sem.at[0]),
        pltpu.make_async_copy(twiddle_all, twiddle, table_sem.at[1]),
        pltpu.make_async_copy(lanes_all, lanes, table_sem.at[2]),
        pltpu.make_async_copy(lanes_back_all, lanes_back, table_sem.at[3]),
        pltpu.make_async_copy(rows_back_all, rows_back, table_sem.at[4]),
    ]
    for load in loads:
        load.start()

    barrier = pltpu.get_barrier_semaphore()

    def greet(step, carry):
        other = jnp.bitwise_xor(chip, step) * 2 + core
        pl.semaphore_signal(barrier, inc=1, device_id={"seq": other}, device_id_type=MESH)
        return carry

    lax.fori_loop(1, CHIPS, greet, 0)
    for other in (sibling, partner):
        pl.semaphore_signal(barrier, inc=1, device_id=other, device_id_type=MESH)

    def roll(q):
        raws[q].wait()
        for n in range(ROWS):
            rolled[q, :, n, :] = raw[q, :, n * COLS : (n + 1) * COLS]

    def slot(q):
        return x.at[min(q, 1), chip, core]

    def own(q):
        return pltpu.make_async_copy(rolled.at[q, channel], slot(q), own_sem.at[q])

    def scatter(q):
        def one(step, carry):
            other = jnp.bitwise_xor(chip, step)
            block = rolled.at[q, jnp.bitwise_xor(other, flip)]
            device = {"seq": other * 2 + goals[q]}
            remote(block, slot(q), send_sem.at[q], recv_sem.at[min(q, 1)], device).start()
            return carry

        lax.fori_loop(1, CHIPS, one, 0)
        if q == 0:
            own(q).start()
            return

        @pl.when(core == goals[q])
        def _():
            own(q).start()

        @pl.when(core != goals[q])
        def _():
            remote(rolled.at[q, channel], slot(q), send_sem.at[q], recv_sem.at[1], sibling).start()

    def wait_blocks(count, sem):
        ref = bulk.at[pl.ds(0, count)]
        pltpu.make_async_copy(ref, ref, sem).wait()

    def sent(q):
        if q == 0:
            wait_blocks(CHIPS - 1, send_sem.at[0])
            return

        @pl.when(core == goals[q])
        def _():
            wait_blocks(CHIPS - 1, send_sem.at[q])

        @pl.when(core != goals[q])
        def _():
            wait_blocks(CHIPS, send_sem.at[q])

    def passing():
        half = x.at[0, :, core]
        return remote(half, half, pass_send, pass_recv, sibling)

    def place(owner, piece, i):
        diagonal = owner + 2 * lax.rem(piece // 2 + channel // 8, 2)
        return i * 8 + lax.rem(piece + channel // 4, 2) * 4 + lax.rem(diagonal + 4 - i, 4)

    def far_start(piece):
        for i in range(4):
            block = part.at[place(1 - group, piece, i)]
            remote(block, far.at[piece, i], far_send.at[piece], far_recv.at[piece], partner).start()

    def far_wait(piece, sem):
        ref = far.at[piece]
        pltpu.make_async_copy(ref, ref, sem.at[piece]).wait()

    def far_next(piece):
        far_wait(piece - 1, far_send)
        far_start(piece)

    def settle(piece):
        far_wait(piece, far_recv)

        def one(i, carry):
            other = place(group, piece, i)
            part[other] = part[other] + far[piece, i]
            for half in range(2):
                block, goal = part.at[other, half], landed.at[1, channel]
                if half == 0:
                    remote(block, goal, out_send.at[1], out_recv.at[1], {"seq": other * 2 + half}).start()
                else:

                    @pl.when(other != chip)
                    def _():
                        remote(block, goal, out_send.at[1], out_recv.at[1], {"seq": other * 2 + half}).start()

                    @pl.when(other == chip)
                    def _():
                        pltpu.make_async_copy(block, goal, out_own).start()

                device = {"dp": 1 - group, "seq": other * 2 + half}
                remote(block, goal, out_send.at[1], out_recv.at[1], device).start()
            return carry

        lax.fori_loop(0, 4, one, 0)

    def gradient(step, carry):
        other = jnp.bitwise_xor(chip, step)
        for half in range(2):
            device = {"seq": other * 2 + half}
            remote(part.at[other, half], landed.at[0, channel], out_send.at[0], out_recv.at[0], device).start()
        return carry

    own_out = pltpu.make_async_copy(part.at[chip, core], landed.at[core, channel], out_own)

    roll(0)
    pl.semaphore_wait(barrier, CHIPS + 1)
    scatter(0)
    pl.semaphore_signal(ready, inc=1, device_id=sibling, device_id_type=MESH)
    roll(1)
    roll(2)
    pl.semaphore_wait(ready, 1)
    sent(0)
    scatter(1)
    own(0).wait()
    wait_blocks(CHIPS - 1, recv_sem.at[0])
    passing().start()
    for load in loads:
        load.wait()
    passing().wait_recv()
    forward(x.at[0], rows, twiddle, lanes, work, spec.at[0])
    sent(1)
    scatter(2)

    @pl.when(core == 0)
    def _():
        own(2).wait()

    @pl.when(core == 1)
    def _():
        own(1).wait()

    wait_blocks(2 * CHIPS - 1, recv_sem.at[1])
    forward(x.at[1], rows, twiddle, lanes, work, spec.at[1])
    backward(spec.at[0], spec.at[1], rows_back, twiddle, lanes_back, wide, part)

    @pl.when(core == 0)
    def _():
        own_out.start()
        remote(part.at[chip, 1], landed.at[0, channel], out_send.at[0], out_recv.at[0], sibling).start()
        lax.fori_loop(1, CHIPS, gradient, 0)

    @pl.when(core == 1)
    def _():
        far_start(0)
        for piece in range(4):
            if piece < 3:
                far_next(piece + 1)
            settle(piece)
        far_wait(3, far_send)

    passing().wait_send()
    sent(2)

    @pl.when(core == 0)
    def _():
        own_out.wait()
        wait_blocks(2 * CHIPS - 1, out_send.at[0])
        wait_blocks(CHIPS - 1, out_recv.at[0])

    @pl.when(core == 1)
    def _():
        wait_blocks(CHIPS, out_recv.at[0])

        @pl.when(side == group)
        def _():
            own_out.wait()
            wait_blocks(2 * CHIPS - 1, out_send.at[1])

        @pl.when(side != group)
        def _():
            wait_blocks(2 * CHIPS, out_send.at[1])

    @pl.when(jnp.logical_and(core == 1, side == group))
    def _():
        wait_blocks(CHIPS - 1, out_recv.at[1])

    @pl.when(jnp.logical_or(core == 0, side != group))
    def _():
        wait_blocks(CHIPS, out_recv.at[1])


def finish(landed, grad, skip, grad_in, filter_grad):
    channels = grad.shape[0]
    shape = (channels, skip.shape[1])
    chosen = lax.broadcasted_iota(jnp.int32, shape, 1) == (
        lax.broadcasted_iota(jnp.int32, shape, 0) + pl.program_id(0) * channels
    )
    gain = jnp.sum(jnp.where(chosen, skip[...], 0.0), axis=1, keepdims=True)
    for n in range(ROWS):
        at = slice(n * COLS, (n + 1) * COLS)
        grad_in[:, at] = landed[0, :, n, :] + gain * grad[:, at]
        filter_grad[:, at] = landed[1, :, n, :]


def shards(inputs, grad_out, filters, skip):
    channels, length = filters.shape
    constants = tables()
    vmem, dma = pltpu.VMEM, pltpu.SemaphoreType.DMA
    any_space = pl.BlockSpec(memory_space=pl.ANY)
    grad = grad_out.reshape(channels, length)
    landed = pl.pallas_call(
        kernel,
        out_shape=jax.ShapeDtypeStruct((2, CHIPS, ROWS, COLS), jnp.float32),
        in_specs=[any_space] * 8,
        out_specs=any_space,
        scratch_shapes=[
            vmem((3, channels, length), jnp.float32),
            vmem((3, CHIPS, ROWS, COLS), jnp.float32),
            vmem((2, CHIPS, 2, ROWS, COLS), jnp.float32),
            vmem((2, 2, 4, 4 * RAD, 2 * RAD), jnp.float32),
            vmem((2, 2, 4 * RAD, COLS), jnp.float32),
            vmem((2, 4, 2, 2 * RAD, COLS), jnp.bfloat16),
            vmem((CHIPS, 2, ROWS, COLS), jnp.float32),
            vmem((4, 4, 2, ROWS, COLS), jnp.float32),
            vmem(constants[0].shape, jnp.bfloat16),
            vmem(constants[1].shape, jnp.bfloat16),
            vmem(constants[2].shape, jnp.float32),
            vmem(constants[3].shape, jnp.bfloat16),
            vmem(constants[4].shape, jnp.bfloat16),
            dma((5,)), dma((3,)), dma((3,)), dma((3,)), dma((2,)), dma(()), dma(()), pltpu.SemaphoreType.REGULAR,
            dma((4,)), dma((4,)), dma((2,)), dma((2,)), dma(()),
        ],
        compiler_params=pltpu.CompilerParams(
            collective_id=0, has_side_effects=True, vmem_limit_bytes=56 * 2**20
        ),
        cost_estimate=pl.CostEstimate(flops=11 * 10**9, bytes_accessed=2 * 10**7, transcendentals=0),
    )(
        grad, inputs.reshape(channels, length), filters,
        *(jnp.asarray(table) for table in constants),
    )
    flat = pl.BlockSpec((16, length), lambda i: (i, 0))
    grad_in, filter_grad = pl.pallas_call(
        finish,
        out_shape=[jax.ShapeDtypeStruct((channels, length), jnp.float32)] * 2,
        grid=(channels // 16,),
        in_specs=[
            pl.BlockSpec((2, 16, ROWS, COLS), lambda i: (0, i, 0, 0)),
            flat,
            pl.BlockSpec((1, channels), lambda i: (0, 0)),
        ],
        out_specs=[flat, flat],
        cost_estimate=pl.CostEstimate(flops=10**6, bytes_accessed=5 * 2**20, transcendentals=0),
    )(landed, grad, skip.reshape(1, channels))
    return (grad_in.reshape(1, channels, length), filter_grad)


def solution(mesh):
    return jax.shard_map(
        shards,
        mesh=mesh,
        in_specs=(P("dp", None, "seq"), P("dp", None, "seq"), P(None, "seq"), P()),
        out_specs=(P("dp", None, "seq"), P(None, "seq")),
        check_vma=False,
    )
```

```python
import functools
import math

import jax
import jax.numpy as jnp
import ml_dtypes
import numpy as np
from jax import lax
from jax.experimental import pallas as pl
from jax.experimental.pallas import tpu as pltpu
from jax.sharding import PartitionSpec as P

MESH = pl.DeviceIdType.MESH
CHIPS = 32
ROWS = 16
COLS = 512
RAD = 128
LENGTH = CHIPS * 2 * ROWS * COLS


def two_parts(matrix):
    high = matrix.astype(ml_dtypes.bfloat16)
    low = (matrix - high.astype(np.float64)).astype(ml_dtypes.bfloat16)
    return high, low


def left_blocks(matrix):
    high, low = two_parts(matrix)
    return np.concatenate([high, low, high], axis=-1)


def right_blocks(matrix):
    high, low = two_parts(matrix)
    return np.concatenate([high, low, high], axis=-2)


@functools.cache
def tables():
    core = np.arange(2)[:, None, None, None]
    branch = np.arange(4)[None, :, None, None]
    freq = 8 * np.arange(RAD)[None, None, :, None] + core + 2 * branch
    row = np.arange(RAD)[None, None, None, :]
    angle = -2.0 * math.pi / 4096.0 * ((4 * freq + 1) * row % 4096)
    cos, sin = np.cos(angle), np.sin(angle)
    rows = np.concatenate([np.concatenate([cos, -sin], -1), np.concatenate([sin, cos], -1)], -2)
    scale = 1.0 / (LENGTH * math.sqrt(LENGTH))
    rows_back = np.swapaxes(rows, -1, -2) * scale
    column = np.arange(COLS)[None, None, None, :]
    angle = -2.0 * math.pi / (4 * LENGTH) * ((4 * freq + 1) * column % (4 * LENGTH))
    twiddle = np.stack([np.cos(angle), np.sin(angle)], axis=1).astype(np.float32)
    inner = np.arange(RAD)[None, :, None]
    outer = 4 * np.arange(RAD)[None, None, :] + np.arange(4)[:, None, None]
    angle = -2.0 * math.pi / COLS * (outer * inner % COLS)
    cos, sin = np.cos(angle), np.sin(angle)
    lanes = np.concatenate([np.concatenate([cos, sin], -1), np.concatenate([-sin, cos], -1)], -2)
    lanes_back = np.swapaxes(lanes, -1, -2)
    return (
        left_blocks(rows),
        left_blocks(rows_back),
        twiddle.reshape(2, 2, 4 * RAD, COLS),
        right_blocks(lanes),
        right_blocks(lanes_back),
    )


def split(value):
    high = value.astype(jnp.bfloat16)
    low = (value - high.astype(jnp.float32)).astype(jnp.bfloat16)
    return high, low


def butterfly(parts, sign):
    (ar, ai), (br, bi), (cr, ci), (dr, di) = parts
    pr, pi, mr, mi = ar + cr, ai + ci, ar - cr, ai - ci
    qr, qi, nr, ni = br + dr, bi + di, br - dr, bi - di
    first = (mr - sign * ni, mi + sign * nr)
    third = (mr + sign * ni, mi - sign * nr)
    return [(pr + qr, pi + qi), first, (pr - qr, pi - qi), third]


def turns(half):
    angles = [-2.0 * math.pi * j * (half + 0.25) / 8.0 for j in range(8)]
    return [(math.cos(angle), math.sin(angle)) for angle in angles]


def dot(left, right):
    return lax.dot_general(left, right, (((1,), (0,)), ((), ())), preferred_element_type=jnp.float32)


def forward(x, rows, twiddle, lanes, work, spec):
    real = [x[4 * j : 4 * j + 4].reshape(RAD, COLS) for j in range(8)]
    for half in range(2):
        factors = turns(half)
        parts = []
        for j in range(4):
            (ar, ai), (br, bi) = factors[j], factors[j + 4]
            parts.append((ar * real[j] + br * real[j + 4], ai * real[j] + bi * real[j + 4]))
        for branch, (re, im) in enumerate(butterfly(parts, -1.0)):
            high, low = split(jnp.concatenate([re, im], axis=0))
            out = dot(rows[half, branch], jnp.concatenate([high, high, low], axis=0))
            re, im = out[:RAD], out[RAD:]
            at = slice(branch * RAD, (branch + 1) * RAD)
            cos, sin = twiddle[half, 0, at], twiddle[half, 1, at]
            work[half, 0, at] = re * cos - im * sin
            work[half, 1, at] = re * sin + im * cos

    def bands(half, carry):
        parts = [
            (work[half, 0, :, RAD * j : RAD * (j + 1)], work[half, 1, :, RAD * j : RAD * (j + 1)]) for j in range(4)
        ]
        for branch, (re, im) in enumerate(butterfly(parts, -1.0)):
            high, low = split(jnp.concatenate([re, im], axis=1))
            spec[half, branch] = dot(jnp.concatenate([high, high, low], axis=1), lanes[branch])
        return carry

    lax.fori_loop(0, 2, bands, 0)


def backward(left, right, rows_back, twiddle, lanes_back, wide, out):
    def bands(half, carry):
        parts = []
        for branch in range(4):
            lr, li = left[half, branch, :, :RAD], left[half, branch, :, RAD:]
            rr, ri = right[half, branch, :, :RAD], right[half, branch, :, RAD:]
            high, low = split(jnp.concatenate([lr * rr + li * ri, li * rr - lr * ri], axis=1))
            back = dot(jnp.concatenate([high, high, low], axis=1), lanes_back[branch])
            parts.append((back[:, :RAD], back[:, RAD:]))
        for j, (re, im) in enumerate(butterfly(parts, 1.0)):
            cols = slice(RAD * j, RAD * (j + 1))
            cos, sin = twiddle[half, 0, :, cols], twiddle[half, 1, :, cols]
            for side, value in enumerate((re * cos + im * sin, im * cos - re * sin)):
                high, low = split(value.reshape(4, RAD, RAD))
                wide[half, :, 0, side * RAD : (side + 1) * RAD, cols] = high
                wide[half, :, 1, side * RAD : (side + 1) * RAD, cols] = low
        return carry

    lax.fori_loop(0, 2, bands, 0)
    values = [0.0] * 8
    for half in range(2):
        factors = turns(half)
        parts = []
        for branch in range(4):
            high, low = wide[half, branch, 0], wide[half, branch, 1]
            back = dot(rows_back[half, branch], jnp.concatenate([high, high, low], axis=0))
            parts.append((back[:RAD], back[RAD:]))
        sums = butterfly(parts, 1.0)
        for j in range(8):
            re, im = sums[j % 4]
            values[j] = values[j] + (factors[j][0] * re + factors[j][1] * im)
    for j in range(8):
        out[4 * j : 4 * j + 4] = values[j].reshape(4, 2, ROWS, COLS)


def kernel(
    grad, inputs, filters, rows_all, rows_back_all, twiddle_all, lanes_all, lanes_back_all,
    landed,
    raw, rolled, x, spec, work, wide, part, far, rows, rows_back, twiddle, lanes, lanes_back,
    table_sem, raw_sem, own_sem, send_sem, recv_sem, pass_send, pass_recv, ready, far_send, far_recv,
    out_send, out_recv, out_own,
):
    me, group = lax.axis_index("seq"), lax.axis_index("dp")
    core, chip = lax.rem(me, 2), me // 2
    side = lax.rem(chip // 8 + chip, 2)
    flip = 4 * group
    channel = jnp.bitwise_xor(chip, flip)
    sibling = {"seq": chip * 2 + 1 - core}
    partner = {"dp": 1 - group, "seq": jnp.bitwise_xor(chip, 4) * 2 + core}
    signals = (grad, inputs, filters)
    bulk = rolled.reshape(3 * CHIPS, ROWS, COLS)
    goals = (core, 1, 0)

    def remote(src, dst, send, recv, device):
        return pltpu.make_async_remote_copy(
            src_ref=src, dst_ref=dst, send_sem=send, recv_sem=recv, device_id=device, device_id_type=MESH
        )

    raws = [pltpu.make_async_copy(signals[q], raw.at[q], raw_sem.at[q]) for q in range(3)]
    for copy in raws:
        copy.start()
    loads = [
        pltpu.make_async_copy(rows_all, rows, table_sem.at[0]),
        pltpu.make_async_copy(twiddle_all, twiddle, table_sem.at[1]),
        pltpu.make_async_copy(lanes_all, lanes, table_sem.at[2]),
        pltpu.make_async_copy(lanes_back_all, lanes_back, table_sem.at[3]),
        pltpu.make_async_copy(rows_back_all, rows_back, table_sem.at[4]),
    ]
    for load in loads:
        load.start()

    barrier = pltpu.get_barrier_semaphore()

    def greet(step, carry):
        other = jnp.bitwise_xor(chip, step) * 2 + core
        pl.semaphore_signal(barrier, inc=1, device_id={"seq": other}, device_id_type=MESH)
        return carry

    lax.fori_loop(1, CHIPS, greet, 0)
    for other in (sibling, partner):
        pl.semaphore_signal(barrier, inc=1, device_id=other, device_id_type=MESH)

    def roll(q):
        raws[q].wait()
        for n in range(ROWS):
            rolled[q, :, n, :] = raw[q, :, n * COLS : (n + 1) * COLS]

    def slot(q):
        return x.at[min(q, 1), chip, core]

    def own(q):
        return pltpu.make_async_copy(rolled.at[q, channel], slot(q), own_sem.at[q])

    def scatter(q):
        def one(step, carry):
            other = jnp.bitwise_xor(chip, lax.rem(step * 11, CHIPS))
            block = rolled.at[q, jnp.bitwise_xor(other, flip)]
            device = {"seq": other * 2 + goals[q]}
            remote(block, slot(q), send_sem.at[q], recv_sem.at[min(q, 1)], device).start()
            return carry

        lax.fori_loop(1, CHIPS, one, 0)
        if q == 0:
            own(q).start()
            return

        @pl.when(core == goals[q])
        def _():
            own(q).start()

        @pl.when(core != goals[q])
        def _():
            remote(rolled.at[q, channel], slot(q), send_sem.at[q], recv_sem.at[1], sibling).start()

    def wait_blocks(count, sem):
        ref = bulk.at[pl.ds(0, count)]
        pltpu.make_async_copy(ref, ref, sem).wait()

    def sent(q):
        if q == 0:
            wait_blocks(CHIPS - 1, send_sem.at[0])
            return

        @pl.when(core == goals[q])
        def _():
            wait_blocks(CHIPS - 1, send_sem.at[q])

        @pl.when(core != goals[q])
        def _():
            wait_blocks(CHIPS, send_sem.at[q])

    def passing():
        half = x.at[0, :, core]
        return remote(half, half, pass_send, pass_recv, sibling)

    def place(owner, piece, i):
        diagonal = owner + 2 * lax.rem(piece // 2 + channel // 8, 2)
        return i * 8 + lax.rem(piece + channel // 4, 2) * 4 + lax.rem(diagonal + 4 - i, 4)

    def far_start(piece):
        for i in range(4):
            block = part.at[place(1 - group, piece, i)]
            remote(block, far.at[piece, i], far_send.at[piece], far_recv.at[piece], partner).start()

    def far_wait(piece, sem):
        ref = far.at[piece]
        pltpu.make_async_copy(ref, ref, sem.at[piece]).wait()

    def far_next(piece):
        far_wait(piece - 1, far_send)
        far_start(piece)

    def settle(piece):
        far_wait(piece, far_recv)

        def add(i, carry):
            other = place(group, piece, i)
            part[other] = part[other] + far[piece, i]
            return carry

        def one(step, carry):
            other = place(group, piece, lax.rem(step + chip // 8, 4))
            half = step // 4
            block, goal = part.at[other, half], landed.at[1, channel]
            device = {"dp": 1 - group, "seq": other * 2 + half}
            remote(block, goal, out_send.at[1], out_recv.at[1], device).start()
            mine = jnp.logical_and(other == chip, half == 1)

            @pl.when(jnp.logical_not(mine))
            def _():
                remote(block, goal, out_send.at[1], out_recv.at[1], {"seq": other * 2 + half}).start()

            @pl.when(mine)
            def _():
                pltpu.make_async_copy(block, goal, out_own).start()

            return carry

        lax.fori_loop(0, 4, add, 0)
        lax.fori_loop(0, 8, one, 0)

    def gradient(step, carry):
        other = jnp.bitwise_xor(chip, lax.rem((1 + lax.rem(step, CHIPS - 1)) * 11, CHIPS))
        half = step // (CHIPS - 1)
        block = part.at[other, half]
        remote(block, landed.at[0, channel], out_send.at[0], out_recv.at[0], {"seq": other * 2 + half}).start()
        return carry

    own_out = pltpu.make_async_copy(part.at[chip, core], landed.at[core, channel], out_own)

    roll(0)
    pl.semaphore_wait(barrier, CHIPS + 1)
    scatter(0)
    pl.semaphore_signal(ready, inc=1, device_id=sibling, device_id_type=MESH)
    roll(1)
    roll(2)
    pl.semaphore_wait(ready, 1)
    sent(0)
    scatter(1)
    own(0).wait()
    wait_blocks(CHIPS - 1, recv_sem.at[0])
    passing().start()
    for load in loads:
        load.wait()
    passing().wait_recv()
    forward(x.at[0], rows, twiddle, lanes, work, spec.at[0])
    sent(1)
    scatter(2)

    @pl.when(core == 0)
    def _():
        own(2).wait()

    @pl.when(core == 1)
    def _():
        own(1).wait()

    wait_blocks(2 * CHIPS - 1, recv_sem.at[1])
    forward(x.at[1], rows, twiddle, lanes, work, spec.at[1])
    backward(spec.at[0], spec.at[1], rows_back, twiddle, lanes_back, wide, part)

    @pl.when(core == 0)
    def _():
        own_out.start()
        remote(part.at[chip, 1], landed.at[0, channel], out_send.at[0], out_recv.at[0], sibling).start()
        lax.fori_loop(0, 2 * CHIPS - 2, gradient, 0)

    @pl.when(core == 1)
    def _():
        far_start(0)
        for piece in range(4):
            if piece < 3:
                far_next(piece + 1)
            settle(piece)
        far_wait(3, far_send)

    passing().wait_send()
    sent(2)

    @pl.when(core == 0)
    def _():
        own_out.wait()
        wait_blocks(2 * CHIPS - 1, out_send.at[0])
        wait_blocks(CHIPS - 1, out_recv.at[0])

    @pl.when(core == 1)
    def _():
        wait_blocks(CHIPS, out_recv.at[0])

        @pl.when(side == group)
        def _():
            own_out.wait()
            wait_blocks(2 * CHIPS - 1, out_send.at[1])

        @pl.when(side != group)
        def _():
            wait_blocks(2 * CHIPS, out_send.at[1])

    @pl.when(jnp.logical_and(core == 1, side == group))
    def _():
        wait_blocks(CHIPS - 1, out_recv.at[1])

    @pl.when(jnp.logical_or(core == 0, side != group))
    def _():
        wait_blocks(CHIPS, out_recv.at[1])


def finish(landed, grad, skip, grad_in, filter_grad):
    channels = grad.shape[0]
    shape = (channels, skip.shape[1])
    chosen = lax.broadcasted_iota(jnp.int32, shape, 1) == (
        lax.broadcasted_iota(jnp.int32, shape, 0) + pl.program_id(0) * channels
    )
    gain = jnp.sum(jnp.where(chosen, skip[...], 0.0), axis=1, keepdims=True)
    for n in range(ROWS):
        at = slice(n * COLS, (n + 1) * COLS)
        grad_in[:, at] = landed[0, :, n, :] + gain * grad[:, at]
        filter_grad[:, at] = landed[1, :, n, :]


def shards(inputs, grad_out, filters, skip):
    channels, length = filters.shape
    constants = tables()
    vmem, dma = pltpu.VMEM, pltpu.SemaphoreType.DMA
    any_space = pl.BlockSpec(memory_space=pl.ANY)
    grad = grad_out.reshape(channels, length)
    landed = pl.pallas_call(
        kernel,
        out_shape=jax.ShapeDtypeStruct((2, CHIPS, ROWS, COLS), jnp.float32),
        in_specs=[any_space] * 8,
        out_specs=any_space,
        scratch_shapes=[
            vmem((3, channels, length), jnp.float32),
            vmem((3, CHIPS, ROWS, COLS), jnp.float32),
            vmem((2, CHIPS, 2, ROWS, COLS), jnp.float32),
            vmem((2, 2, 4, 4 * RAD, 2 * RAD), jnp.float32),
            vmem((2, 2, 4 * RAD, COLS), jnp.float32),
            vmem((2, 4, 2, 2 * RAD, COLS), jnp.bfloat16),
            vmem((CHIPS, 2, ROWS, COLS), jnp.float32),
            vmem((4, 4, 2, ROWS, COLS), jnp.float32),
            vmem(constants[0].shape, jnp.bfloat16),
            vmem(constants[1].shape, jnp.bfloat16),
            vmem(constants[2].shape, jnp.float32),
            vmem(constants[3].shape, jnp.bfloat16),
            vmem(constants[4].shape, jnp.bfloat16),
            dma((5,)), dma((3,)), dma((3,)), dma((3,)), dma((2,)), dma(()), dma(()), pltpu.SemaphoreType.REGULAR,
            dma((4,)), dma((4,)), dma((2,)), dma((2,)), dma(()),
        ],
        compiler_params=pltpu.CompilerParams(
            collective_id=0, has_side_effects=True, vmem_limit_bytes=56 * 2**20
        ),
        cost_estimate=pl.CostEstimate(flops=11 * 10**9, bytes_accessed=2 * 10**7, transcendentals=0),
    )(
        grad, inputs.reshape(channels, length), filters,
        *(jnp.asarray(table) for table in constants),
    )
    flat = pl.BlockSpec((16, length), lambda i: (i, 0))
    grad_in, filter_grad = pl.pallas_call(
        finish,
        out_shape=[jax.ShapeDtypeStruct((channels, length), jnp.float32)] * 2,
        grid=(channels // 16,),
        in_specs=[
            pl.BlockSpec((2, 16, ROWS, COLS), lambda i: (0, i, 0, 0)),
            flat,
            pl.BlockSpec((1, channels), lambda i: (0, 0)),
        ],
        out_specs=[flat, flat],
        cost_estimate=pl.CostEstimate(flops=10**6, bytes_accessed=5 * 2**20, transcendentals=0),
    )(landed, grad, skip.reshape(1, channels))
    return (grad_in.reshape(1, channels, length), filter_grad)


def solution(mesh):
    return jax.shard_map(
        shards,
        mesh=mesh,
        in_specs=(P("dp", None, "seq"), P("dp", None, "seq"), P(None, "seq"), P()),
        out_specs=(P("dp", None, "seq"), P(None, "seq")),
        check_vma=False,
    )
```

```python
import functools
import math

import jax
import jax.numpy as jnp
import ml_dtypes
import numpy as np
from jax import lax
from jax.experimental import pallas as pl
from jax.experimental.pallas import tpu as pltpu
from jax.sharding import PartitionSpec as P

MESH = pl.DeviceIdType.MESH
CHIPS = 32
ROWS = 16
COLS = 512
RAD = 128
LENGTH = CHIPS * 2 * ROWS * COLS


def two_parts(matrix):
    high = matrix.astype(ml_dtypes.bfloat16)
    low = (matrix - high.astype(np.float64)).astype(ml_dtypes.bfloat16)
    return high, low


def left_blocks(matrix):
    high, low = two_parts(matrix)
    return np.concatenate([high, low, high], axis=-1)


def right_blocks(matrix):
    high, low = two_parts(matrix)
    return np.concatenate([high, low, high], axis=-2)


@functools.cache
def tables():
    core = np.arange(2)[:, None, None, None]
    branch = np.arange(4)[None, :, None, None]
    freq = 8 * np.arange(RAD)[None, None, :, None] + core + 2 * branch
    row = np.arange(RAD)[None, None, None, :]
    angle = -2.0 * math.pi / 4096.0 * ((4 * freq + 1) * row % 4096)
    cos, sin = np.cos(angle), np.sin(angle)
    rows = np.concatenate([np.concatenate([cos, -sin], -1), np.concatenate([sin, cos], -1)], -2)
    scale = 1.0 / (LENGTH * math.sqrt(LENGTH))
    rows_back = np.swapaxes(rows, -1, -2) * scale
    column = np.arange(COLS)[None, None, None, :]
    angle = -2.0 * math.pi / (4 * LENGTH) * ((4 * freq + 1) * column % (4 * LENGTH))
    twiddle = np.stack([np.cos(angle), np.sin(angle)], axis=1).astype(np.float32)
    inner = np.arange(RAD)[None, :, None]
    outer = 4 * np.arange(RAD)[None, None, :] + np.arange(4)[:, None, None]
    angle = -2.0 * math.pi / COLS * (outer * inner % COLS)
    cos, sin = np.cos(angle), np.sin(angle)
    lanes = np.concatenate([np.concatenate([cos, sin], -1), np.concatenate([-sin, cos], -1)], -2)
    lanes_back = np.swapaxes(lanes, -1, -2)
    return (
        left_blocks(rows),
        left_blocks(rows_back),
        twiddle.reshape(2, 2, 4 * RAD, COLS),
        right_blocks(lanes),
        right_blocks(lanes_back),
    )


def split(value):
    high = value.astype(jnp.bfloat16)
    low = (value - high.astype(jnp.float32)).astype(jnp.bfloat16)
    return high, low


def butterfly(parts, sign):
    (ar, ai), (br, bi), (cr, ci), (dr, di) = parts
    pr, pi, mr, mi = ar + cr, ai + ci, ar - cr, ai - ci
    qr, qi, nr, ni = br + dr, bi + di, br - dr, bi - di
    first = (mr - sign * ni, mi + sign * nr)
    third = (mr + sign * ni, mi - sign * nr)
    return [(pr + qr, pi + qi), first, (pr - qr, pi - qi), third]


def turns(half):
    angles = [-2.0 * math.pi * j * (half + 0.25) / 8.0 for j in range(8)]
    return [(math.cos(angle), math.sin(angle)) for angle in angles]


def dot(left, right):
    return lax.dot_general(left, right, (((1,), (0,)), ((), ())), preferred_element_type=jnp.float32)


def forward(x, rows, twiddle, lanes, work, spec):
    real = [x[4 * j : 4 * j + 4].reshape(RAD, COLS) for j in range(8)]
    for half in range(2):
        factors = turns(half)
        parts = []
        for j in range(4):
            (ar, ai), (br, bi) = factors[j], factors[j + 4]
            parts.append((ar * real[j] + br * real[j + 4], ai * real[j] + bi * real[j + 4]))
        for branch, (re, im) in enumerate(butterfly(parts, -1.0)):
            high, low = split(jnp.concatenate([re, im], axis=0))
            out = dot(rows[half, branch], jnp.concatenate([high, high, low], axis=0))
            re, im = out[:RAD], out[RAD:]
            at = slice(branch * RAD, (branch + 1) * RAD)
            cos, sin = twiddle[half, 0, at], twiddle[half, 1, at]
            work[half, 0, at] = re * cos - im * sin
            work[half, 1, at] = re * sin + im * cos

    def bands(half, carry):
        parts = [
            (work[half, 0, :, RAD * j : RAD * (j + 1)], work[half, 1, :, RAD * j : RAD * (j + 1)]) for j in range(4)
        ]
        for branch, (re, im) in enumerate(butterfly(parts, -1.0)):
            high, low = split(jnp.concatenate([re, im], axis=1))
            spec[half, branch] = dot(jnp.concatenate([high, high, low], axis=1), lanes[branch])
        return carry

    lax.fori_loop(0, 2, bands, 0)


def backward(left, right, rows_back, twiddle, lanes_back, wide, out):
    def bands(half, carry):
        parts = []
        for branch in range(4):
            lr, li = left[half, branch, :, :RAD], left[half, branch, :, RAD:]
            rr, ri = right[half, branch, :, :RAD], right[half, branch, :, RAD:]
            high, low = split(jnp.concatenate([lr * rr + li * ri, li * rr - lr * ri], axis=1))
            back = dot(jnp.concatenate([high, high, low], axis=1), lanes_back[branch])
            parts.append((back[:, :RAD], back[:, RAD:]))
        for j, (re, im) in enumerate(butterfly(parts, 1.0)):
            cols = slice(RAD * j, RAD * (j + 1))
            cos, sin = twiddle[half, 0, :, cols], twiddle[half, 1, :, cols]
            for side, value in enumerate((re * cos + im * sin, im * cos - re * sin)):
                high, low = split(value.reshape(4, RAD, RAD))
                wide[half, :, 0, side * RAD : (side + 1) * RAD, cols] = high
                wide[half, :, 1, side * RAD : (side + 1) * RAD, cols] = low
        return carry

    lax.fori_loop(0, 2, bands, 0)
    values = [0.0] * 8
    for half in range(2):
        factors = turns(half)
        parts = []
        for branch in range(4):
            high, low = wide[half, branch, 0], wide[half, branch, 1]
            back = dot(rows_back[half, branch], jnp.concatenate([high, high, low], axis=0))
            parts.append((back[:RAD], back[RAD:]))
        sums = butterfly(parts, 1.0)
        for j in range(8):
            re, im = sums[j % 4]
            values[j] = values[j] + (factors[j][0] * re + factors[j][1] * im)
    for j in range(8):
        out[4 * j : 4 * j + 4] = values[j].reshape(4, 2, ROWS, COLS)


def kernel(
    grad, inputs, filters, rows_all, rows_back_all, twiddle_all, lanes_all, lanes_back_all,
    landed,
    raw, rolled, x, spec, work, wide, part, far, rows, rows_back, twiddle, lanes, lanes_back,
    table_sem, raw_sem, own_sem, send_sem, recv_sem, pass_send, pass_recv, ready, far_send, far_recv,
    out_send, out_recv, out_own,
):
    me, group = lax.axis_index("seq"), lax.axis_index("dp")
    core, chip = lax.rem(me, 2), me // 2
    side = lax.rem(chip // 8 + chip, 2)
    flip = 4 * group
    channel = jnp.bitwise_xor(chip, flip)
    sibling = {"seq": chip * 2 + 1 - core}
    partner = {"dp": 1 - group, "seq": jnp.bitwise_xor(chip, 4) * 2 + core}
    signals = (grad, inputs, filters)
    bulk = rolled.reshape(3 * CHIPS, ROWS, COLS)
    goals = (core, 1, 0)

    def remote(src, dst, send, recv, device):
        return pltpu.make_async_remote_copy(
            src_ref=src, dst_ref=dst, send_sem=send, recv_sem=recv, device_id=device, device_id_type=MESH
        )

    raws = [pltpu.make_async_copy(signals[q], raw.at[q], raw_sem.at[q]) for q in range(3)]
    raws[0].start()
    loads = [
        pltpu.make_async_copy(rows_all, rows, table_sem.at[0]),
        pltpu.make_async_copy(twiddle_all, twiddle, table_sem.at[1]),
        pltpu.make_async_copy(lanes_all, lanes, table_sem.at[2]),
        pltpu.make_async_copy(lanes_back_all, lanes_back, table_sem.at[3]),
        pltpu.make_async_copy(rows_back_all, rows_back, table_sem.at[4]),
    ]
    barrier = pltpu.get_barrier_semaphore()

    def greet(step, carry):
        other = jnp.bitwise_xor(chip, CHIPS - step) * 2 + core
        pl.semaphore_signal(barrier, inc=1, device_id={"seq": other}, device_id_type=MESH)
        return carry

    lax.fori_loop(1, CHIPS, greet, 0)
    for other in (sibling, partner):
        pl.semaphore_signal(barrier, inc=1, device_id=other, device_id_type=MESH)
    for copy in raws[1:] + loads:
        copy.start()

    def roll(q):
        raws[q].wait()
        for n in range(ROWS):
            rolled[q, :, n, :] = raw[q, :, n * COLS : (n + 1) * COLS]

    def slot(q):
        return x.at[min(q, 1), chip, core]

    def own(q):
        return pltpu.make_async_copy(rolled.at[q, channel], slot(q), own_sem.at[q])

    def scatter(q):
        def one(step, carry):
            other = jnp.bitwise_xor(chip, lax.rem(step * 11, CHIPS))
            block = rolled.at[q, jnp.bitwise_xor(other, flip)]
            device = {"seq": other * 2 + goals[q]}
            remote(block, slot(q), send_sem.at[q], recv_sem.at[min(q, 1)], device).start()
            return carry

        lax.fori_loop(1, CHIPS, one, 0)
        if q == 0:
            own(q).start()
            return

        @pl.when(core == goals[q])
        def _():
            own(q).start()

        @pl.when(core != goals[q])
        def _():
            remote(rolled.at[q, channel], slot(q), send_sem.at[q], recv_sem.at[1], sibling).start()

    def wait_blocks(count, sem):
        ref = bulk.at[pl.ds(0, count)]
        pltpu.make_async_copy(ref, ref, sem).wait()

    def sent(q):
        if q == 0:
            wait_blocks(CHIPS - 1, send_sem.at[0])
            return

        @pl.when(core == goals[q])
        def _():
            wait_blocks(CHIPS - 1, send_sem.at[q])

        @pl.when(core != goals[q])
        def _():
            wait_blocks(CHIPS, send_sem.at[q])

    def passing():
        half = x.at[0, :, core]
        return remote(half, half, pass_send, pass_recv, sibling)

    def place(owner, piece, i):
        diagonal = owner + 2 * lax.rem(piece // 2 + channel // 8, 2)
        return i * 8 + lax.rem(piece + channel // 4, 2) * 4 + lax.rem(diagonal + 4 - i, 4)

    def far_start(piece):
        for i in range(4):
            block = part.at[place(1 - group, piece, i)]
            remote(block, far.at[piece, i], far_send.at[piece], far_recv.at[piece], partner).start()

    def far_wait(piece, sem):
        ref = far.at[piece]
        pltpu.make_async_copy(ref, ref, sem.at[piece]).wait()

    def far_next(piece):
        far_wait(piece - 1, far_send)
        far_start(piece)

    def settle(piece):
        far_wait(piece, far_recv)

        def add(i, carry):
            other = place(group, piece, i)
            part[other] = part[other] + far[piece, i]
            return carry

        def one(step, carry):
            other = place(group, piece, lax.rem(step + chip // 8, 4))
            half = lax.rem(step // 4 + step, 2)
            block, goal = part.at[other, half], landed.at[1, channel]
            device = {"dp": 1 - group, "seq": other * 2 + half}
            remote(block, goal, out_send.at[1], out_recv.at[1], device).start()
            mine = jnp.logical_and(other == chip, half == 1)

            @pl.when(jnp.logical_not(mine))
            def _():
                remote(block, goal, out_send.at[1], out_recv.at[1], {"seq": other * 2 + half}).start()

            @pl.when(mine)
            def _():
                pltpu.make_async_copy(block, goal, out_own).start()

            return carry

        lax.fori_loop(0, 4, add, 0)
        lax.fori_loop(0, 8, one, 0)

    def gradient(step, carry):
        other = jnp.bitwise_xor(chip, lax.rem((1 + lax.rem(step, CHIPS - 1)) * 11, CHIPS))
        half = lax.rem(step // (CHIPS - 1) + lax.rem(step, CHIPS - 1), 2)
        block = part.at[other, half]
        remote(block, landed.at[0, channel], out_send.at[0], out_recv.at[0], {"seq": other * 2 + half}).start()
        return carry

    own_out = pltpu.make_async_copy(part.at[chip, core], landed.at[core, channel], out_own)

    roll(0)
    pl.semaphore_wait(barrier, CHIPS + 1)
    scatter(0)
    pl.semaphore_signal(ready, inc=1, device_id=sibling, device_id_type=MESH)
    roll(1)
    roll(2)
    pl.semaphore_wait(ready, 1)
    sent(0)
    scatter(1)
    own(0).wait()
    wait_blocks(CHIPS - 1, recv_sem.at[0])
    passing().start()
    for load in loads:
        load.wait()
    passing().wait_recv()
    forward(x.at[0], rows, twiddle, lanes, work, spec.at[0])
    sent(1)
    scatter(2)

    @pl.when(core == 0)
    def _():
        own(2).wait()

    @pl.when(core == 1)
    def _():
        own(1).wait()

    wait_blocks(2 * CHIPS - 1, recv_sem.at[1])
    forward(x.at[1], rows, twiddle, lanes, work, spec.at[1])
    backward(spec.at[0], spec.at[1], rows_back, twiddle, lanes_back, wide, part)

    @pl.when(core == 0)
    def _():
        own_out.start()
        remote(part.at[chip, 1], landed.at[0, channel], out_send.at[0], out_recv.at[0], sibling).start()
        lax.fori_loop(0, 2 * CHIPS - 2, gradient, 0)

    @pl.when(core == 1)
    def _():
        far_start(0)
        for piece in range(4):
            if piece < 3:
                far_next(piece + 1)
            settle(piece)
        far_wait(3, far_send)

    passing().wait_send()
    sent(2)

    @pl.when(core == 0)
    def _():
        own_out.wait()
        wait_blocks(2 * CHIPS - 1, out_send.at[0])
        wait_blocks(CHIPS - 1, out_recv.at[0])

    @pl.when(core == 1)
    def _():
        wait_blocks(CHIPS, out_recv.at[0])

        @pl.when(side == group)
        def _():
            own_out.wait()
            wait_blocks(2 * CHIPS - 1, out_send.at[1])

        @pl.when(side != group)
        def _():
            wait_blocks(2 * CHIPS, out_send.at[1])

    @pl.when(jnp.logical_and(core == 1, side == group))
    def _():
        wait_blocks(CHIPS - 1, out_recv.at[1])

    @pl.when(jnp.logical_or(core == 0, side != group))
    def _():
        wait_blocks(CHIPS, out_recv.at[1])


def finish(landed, grad, skip, grad_in, filter_grad):
    channels = grad.shape[0]
    shape = (channels, skip.shape[1])
    chosen = lax.broadcasted_iota(jnp.int32, shape, 1) == (
        lax.broadcasted_iota(jnp.int32, shape, 0) + pl.program_id(0) * channels
    )
    gain = jnp.sum(jnp.where(chosen, skip[...], 0.0), axis=1, keepdims=True)
    for n in range(ROWS):
        at = slice(n * COLS, (n + 1) * COLS)
        grad_in[:, at] = landed[0, :, n, :] + gain * grad[:, at]
        filter_grad[:, at] = landed[1, :, n, :]


def shards(inputs, grad_out, filters, skip):
    channels, length = filters.shape
    constants = tables()
    vmem, dma = pltpu.VMEM, pltpu.SemaphoreType.DMA
    any_space = pl.BlockSpec(memory_space=pl.ANY)
    grad = grad_out.reshape(channels, length)
    landed = pl.pallas_call(
        kernel,
        out_shape=jax.ShapeDtypeStruct((2, CHIPS, ROWS, COLS), jnp.float32),
        in_specs=[any_space] * 8,
        out_specs=any_space,
        scratch_shapes=[
            vmem((3, channels, length), jnp.float32),
            vmem((3, CHIPS, ROWS, COLS), jnp.float32),
            vmem((2, CHIPS, 2, ROWS, COLS), jnp.float32),
            vmem((2, 2, 4, 4 * RAD, 2 * RAD), jnp.float32),
            vmem((2, 2, 4 * RAD, COLS), jnp.float32),
            vmem((2, 4, 2, 2 * RAD, COLS), jnp.bfloat16),
            vmem((CHIPS, 2, ROWS, COLS), jnp.float32),
            vmem((4, 4, 2, ROWS, COLS), jnp.float32),
            vmem(constants[0].shape, jnp.bfloat16),
            vmem(constants[1].shape, jnp.bfloat16),
            vmem(constants[2].shape, jnp.float32),
            vmem(constants[3].shape, jnp.bfloat16),
            vmem(constants[4].shape, jnp.bfloat16),
            dma((5,)), dma((3,)), dma((3,)), dma((3,)), dma((2,)), dma(()), dma(()), pltpu.SemaphoreType.REGULAR,
            dma((4,)), dma((4,)), dma((2,)), dma((2,)), dma(()),
        ],
        compiler_params=pltpu.CompilerParams(
            collective_id=0, has_side_effects=True, vmem_limit_bytes=56 * 2**20
        ),
        cost_estimate=pl.CostEstimate(flops=11 * 10**9, bytes_accessed=2 * 10**7, transcendentals=0),
    )(
        grad, inputs.reshape(channels, length), filters,
        *(jnp.asarray(table) for table in constants),
    )
    flat = pl.BlockSpec((16, length), lambda i: (i, 0))
    grad_in, filter_grad = pl.pallas_call(
        finish,
        out_shape=[jax.ShapeDtypeStruct((channels, length), jnp.float32)] * 2,
        grid=(channels // 16,),
        in_specs=[
            pl.BlockSpec((2, 16, ROWS, COLS), lambda i: (0, i, 0, 0)),
            flat,
            pl.BlockSpec((1, channels), lambda i: (0, 0)),
        ],
        out_specs=[flat, flat],
        cost_estimate=pl.CostEstimate(flops=10**6, bytes_accessed=5 * 2**20, transcendentals=0),
    )(landed, grad, skip.reshape(1, channels))
    return (grad_in.reshape(1, channels, length), filter_grad)


def solution(mesh):
    return jax.shard_map(
        shards,
        mesh=mesh,
        in_specs=(P("dp", None, "seq"), P("dp", None, "seq"), P(None, "seq"), P()),
        out_specs=(P("dp", None, "seq"), P(None, "seq")),
        check_vma=False,
    )
```

```python
import functools
import math

import jax
import jax.numpy as jnp
import ml_dtypes
import numpy as np
from jax import lax
from jax.experimental import pallas as pl
from jax.experimental.pallas import tpu as pltpu
from jax.sharding import PartitionSpec as P

MESH = pl.DeviceIdType.MESH
CHIPS = 32
ROWS = 16
COLS = 512
RAD = 128
LENGTH = CHIPS * 2 * ROWS * COLS


def two_parts(matrix):
    high = matrix.astype(ml_dtypes.bfloat16)
    low = (matrix - high.astype(np.float64)).astype(ml_dtypes.bfloat16)
    return high, low


def left_blocks(matrix):
    high, low = two_parts(matrix)
    return np.concatenate([high, low, high], axis=-1)


def right_blocks(matrix):
    high, low = two_parts(matrix)
    return np.concatenate([high, low, high], axis=-2)


@functools.cache
def tables():
    core = np.arange(2)[:, None, None, None]
    branch = np.arange(4)[None, :, None, None]
    freq = 8 * np.arange(RAD)[None, None, :, None] + core + 2 * branch
    row = np.arange(RAD)[None, None, None, :]
    angle = -2.0 * math.pi / 4096.0 * ((4 * freq + 1) * row % 4096)
    cos, sin = np.cos(angle), np.sin(angle)
    rows = np.concatenate([np.concatenate([cos, -sin], -1), np.concatenate([sin, cos], -1)], -2)
    scale = 1.0 / (LENGTH * math.sqrt(LENGTH))
    rows_back = np.swapaxes(rows, -1, -2) * scale
    column = np.arange(COLS)[None, None, None, :]
    angle = -2.0 * math.pi / (4 * LENGTH) * ((4 * freq + 1) * column % (4 * LENGTH))
    twiddle = np.stack([np.cos(angle), np.sin(angle)], axis=1).astype(np.float32)
    inner = np.arange(RAD)[None, :, None]
    outer = 4 * np.arange(RAD)[None, None, :] + np.arange(4)[:, None, None]
    angle = -2.0 * math.pi / COLS * (outer * inner % COLS)
    cos, sin = np.cos(angle), np.sin(angle)
    lanes = np.concatenate([np.concatenate([cos, sin], -1), np.concatenate([-sin, cos], -1)], -2)
    lanes_back = np.swapaxes(lanes, -1, -2)
    return (
        left_blocks(rows),
        left_blocks(rows_back),
        twiddle.reshape(2, 2, 4 * RAD, COLS),
        right_blocks(lanes),
        right_blocks(lanes_back),
    )


def split(value):
    high = value.astype(jnp.bfloat16)
    low = (value - high.astype(jnp.float32)).astype(jnp.bfloat16)
    return high, low


def butterfly(parts, sign):
    (ar, ai), (br, bi), (cr, ci), (dr, di) = parts
    pr, pi, mr, mi = ar + cr, ai + ci, ar - cr, ai - ci
    qr, qi, nr, ni = br + dr, bi + di, br - dr, bi - di
    first = (mr - sign * ni, mi + sign * nr)
    third = (mr + sign * ni, mi - sign * nr)
    return [(pr + qr, pi + qi), first, (pr - qr, pi - qi), third]


def turns(half):
    angles = [-2.0 * math.pi * j * (half + 0.25) / 8.0 for j in range(8)]
    return [(math.cos(angle), math.sin(angle)) for angle in angles]


def dot(left, right):
    return lax.dot_general(left, right, (((1,), (0,)), ((), ())), preferred_element_type=jnp.float32)


def forward(x, rows, twiddle, lanes, work, spec):
    real = [x[4 * j : 4 * j + 4].reshape(RAD, COLS) for j in range(8)]
    for half in range(2):
        factors = turns(half)
        parts = []
        for j in range(4):
            (ar, ai), (br, bi) = factors[j], factors[j + 4]
            parts.append((ar * real[j] + br * real[j + 4], ai * real[j] + bi * real[j + 4]))
        for branch, (re, im) in enumerate(butterfly(parts, -1.0)):
            high, low = split(jnp.concatenate([re, im], axis=0))
            out = dot(rows[half, branch], jnp.concatenate([high, high, low], axis=0))
            re, im = out[:RAD], out[RAD:]
            at = slice(branch * RAD, (branch + 1) * RAD)
            cos, sin = twiddle[half, 0, at], twiddle[half, 1, at]
            work[half, 0, at] = re * cos - im * sin
            work[half, 1, at] = re * sin + im * cos

    def bands(half, carry):
        parts = [
            (work[half, 0, :, RAD * j : RAD * (j + 1)], work[half, 1, :, RAD * j : RAD * (j + 1)]) for j in range(4)
        ]
        for branch, (re, im) in enumerate(butterfly(parts, -1.0)):
            high, low = split(jnp.concatenate([re, im], axis=1))
            spec[half, branch] = dot(jnp.concatenate([high, high, low], axis=1), lanes[branch])
        return carry

    lax.fori_loop(0, 2, bands, 0)


def backward(left, right, rows_back, twiddle, lanes_back, wide, out):
    def bands(half, carry):
        parts = []
        for branch in range(4):
            lr, li = left[half, branch, :, :RAD], left[half, branch, :, RAD:]
            rr, ri = right[half, branch, :, :RAD], right[half, branch, :, RAD:]
            high, low = split(jnp.concatenate([lr * rr + li * ri, li * rr - lr * ri], axis=1))
            back = dot(jnp.concatenate([high, high, low], axis=1), lanes_back[branch])
            parts.append((back[:, :RAD], back[:, RAD:]))
        for j, (re, im) in enumerate(butterfly(parts, 1.0)):
            cols = slice(RAD * j, RAD * (j + 1))
            cos, sin = twiddle[half, 0, :, cols], twiddle[half, 1, :, cols]
            for side, value in enumerate((re * cos + im * sin, im * cos - re * sin)):
                high, low = split(value.reshape(4, RAD, RAD))
                wide[half, :, 0, side * RAD : (side + 1) * RAD, cols] = high
                wide[half, :, 1, side * RAD : (side + 1) * RAD, cols] = low
        return carry

    lax.fori_loop(0, 2, bands, 0)
    values = [0.0] * 8
    for half in range(2):
        factors = turns(half)
        parts = []
        for branch in range(4):
            high, low = wide[half, branch, 0], wide[half, branch, 1]
            back = dot(rows_back[half, branch], jnp.concatenate([high, high, low], axis=0))
            parts.append((back[:RAD], back[RAD:]))
        sums = butterfly(parts, 1.0)
        for j in range(8):
            re, im = sums[j % 4]
            values[j] = values[j] + (factors[j][0] * re + factors[j][1] * im)
    for j in range(8):
        out[4 * j : 4 * j + 4] = values[j].reshape(4, 2, ROWS, COLS)


def kernel(
    grad, inputs, filters, rows_all, rows_back_all, twiddle_all, lanes_all, lanes_back_all,
    landed,
    raw, rolled, x, spec, work, wide, part, far, rows, rows_back, twiddle, lanes, lanes_back,
    table_sem, raw_sem, own_sem, send_sem, recv_sem, pass_send, pass_recv, ready, far_send, far_recv,
    out_send, out_recv, out_own,
):
    me, group = lax.axis_index("seq"), lax.axis_index("dp")
    core, chip = lax.rem(me, 2), me // 2
    side = lax.rem(chip // 8 + chip, 2)
    flip = 4 * group
    channel = jnp.bitwise_xor(chip, flip)
    sibling = {"seq": chip * 2 + 1 - core}
    partner = {"dp": 1 - group, "seq": jnp.bitwise_xor(chip, 4) * 2 + core}
    signals = (grad, inputs, filters)
    bulk = rolled.reshape(3 * CHIPS, ROWS, COLS)
    goals = (core, 1, 0)

    def remote(src, dst, send, recv, device):
        return pltpu.make_async_remote_copy(
            src_ref=src, dst_ref=dst, send_sem=send, recv_sem=recv, device_id=device, device_id_type=MESH
        )

    raws = [pltpu.make_async_copy(signals[q], raw.at[q], raw_sem.at[q]) for q in range(3)]
    raws[0].start()
    loads = [
        pltpu.make_async_copy(rows_all, rows, table_sem.at[0]),
        pltpu.make_async_copy(twiddle_all, twiddle, table_sem.at[1]),
        pltpu.make_async_copy(lanes_all, lanes, table_sem.at[2]),
        pltpu.make_async_copy(lanes_back_all, lanes_back, table_sem.at[3]),
        pltpu.make_async_copy(rows_back_all, rows_back, table_sem.at[4]),
    ]
    barrier = pltpu.get_barrier_semaphore()

    def greet(step, carry):
        other = jnp.bitwise_xor(chip, CHIPS - step) * 2 + core
        pl.semaphore_signal(barrier, inc=1, device_id={"seq": other}, device_id_type=MESH)
        return carry

    lax.fori_loop(1, CHIPS, greet, 0)
    for other in (sibling, partner):
        pl.semaphore_signal(barrier, inc=1, device_id=other, device_id_type=MESH)
    for copy in raws[1:] + loads:
        copy.start()

    def roll(q):
        raws[q].wait()
        for n in range(ROWS):
            rolled[q, :, n, :] = raw[q, :, n * COLS : (n + 1) * COLS]

    def slot(q):
        return x.at[min(q, 1), chip, core]

    def own(q):
        return pltpu.make_async_copy(rolled.at[q, channel], slot(q), own_sem.at[q])

    def scatter(q):
        def one(step, carry):
            other = jnp.bitwise_xor(chip, lax.rem(step * 11, CHIPS))
            block = rolled.at[q, jnp.bitwise_xor(other, flip)]
            device = {"seq": other * 2 + goals[q]}
            remote(block, slot(q), send_sem.at[q], recv_sem.at[min(q, 1)], device).start()
            return carry

        lax.fori_loop(1, CHIPS, one, 0, unroll=True)
        if q == 0:
            own(q).start()
            return

        @pl.when(core == goals[q])
        def _():
            own(q).start()

        @pl.when(core != goals[q])
        def _():
            remote(rolled.at[q, channel], slot(q), send_sem.at[q], recv_sem.at[1], sibling).start()

    def wait_blocks(count, sem):
        ref = bulk.at[pl.ds(0, count)]
        pltpu.make_async_copy(ref, ref, sem).wait()

    def sent(q):
        if q == 0:
            wait_blocks(CHIPS - 1, send_sem.at[0])
            return

        @pl.when(core == goals[q])
        def _():
            wait_blocks(CHIPS - 1, send_sem.at[q])

        @pl.when(core != goals[q])
        def _():
            wait_blocks(CHIPS, send_sem.at[q])

    def passing():
        half = x.at[0, :, core]
        return remote(half, half, pass_send, pass_recv, sibling)

    def place(owner, piece, i):
        diagonal = owner + 2 * lax.rem(piece // 2 + channel // 8, 2)
        return i * 8 + lax.rem(piece + channel // 4, 2) * 4 + lax.rem(diagonal + 4 - i, 4)

    def far_start(piece):
        for i in range(4):
            block = part.at[place(1 - group, piece, i)]
            remote(block, far.at[piece, i], far_send.at[piece], far_recv.at[piece], partner).start()

    def far_wait(piece, sem):
        ref = far.at[piece]
        pltpu.make_async_copy(ref, ref, sem.at[piece]).wait()

    def far_next(piece):
        far_wait(piece - 1, far_send)
        far_start(piece)

    def settle(piece):
        far_wait(piece, far_recv)

        def add(i, carry):
            other = place(group, piece, i)
            part[other] = part[other] + far[piece, i]
            return carry

        def one(step, carry):
            other = place(group, piece, lax.rem(step + chip // 8, 4))
            half = lax.rem(step // 4 + step, 2)
            block, goal = part.at[other, half], landed.at[1, channel]
            device = {"dp": 1 - group, "seq": other * 2 + half}
            remote(block, goal, out_send.at[1], out_recv.at[1], device).start()
            mine = jnp.logical_and(other == chip, half == 1)

            @pl.when(jnp.logical_not(mine))
            def _():
                remote(block, goal, out_send.at[1], out_recv.at[1], {"seq": other * 2 + half}).start()

            @pl.when(mine)
            def _():
                pltpu.make_async_copy(block, goal, out_own).start()

            return carry

        lax.fori_loop(0, 4, add, 0)
        lax.fori_loop(0, 8, one, 0)

    def gradient(step, carry):
        other = jnp.bitwise_xor(chip, lax.rem((1 + lax.rem(step, CHIPS - 1)) * 11, CHIPS))
        half = lax.rem(step // (CHIPS - 1) + lax.rem(step, CHIPS - 1), 2)
        block = part.at[other, half]
        remote(block, landed.at[0, channel], out_send.at[0], out_recv.at[0], {"seq": other * 2 + half}).start()
        return carry

    own_out = pltpu.make_async_copy(part.at[chip, core], landed.at[core, channel], out_own)

    roll(0)
    pl.semaphore_wait(barrier, CHIPS + 1)
    scatter(0)
    pl.semaphore_signal(ready, inc=1, device_id=sibling, device_id_type=MESH)
    roll(1)
    roll(2)
    pl.semaphore_wait(ready, 1)
    sent(0)
    scatter(1)
    own(0).wait()
    wait_blocks(CHIPS - 1, recv_sem.at[0])
    passing().start()
    for load in loads:
        load.wait()
    passing().wait_recv()
    forward(x.at[0], rows, twiddle, lanes, work, spec.at[0])
    sent(1)
    scatter(2)

    @pl.when(core == 0)
    def _():
        own(2).wait()

    @pl.when(core == 1)
    def _():
        own(1).wait()

    wait_blocks(2 * CHIPS - 1, recv_sem.at[1])
    forward(x.at[1], rows, twiddle, lanes, work, spec.at[1])
    backward(spec.at[0], spec.at[1], rows_back, twiddle, lanes_back, wide, part)

    @pl.when(core == 0)
    def _():
        own_out.start()
        remote(part.at[chip, 1], landed.at[0, channel], out_send.at[0], out_recv.at[0], sibling).start()
        lax.fori_loop(0, 2 * CHIPS - 2, gradient, 0)

    @pl.when(core == 1)
    def _():
        far_start(0)
        for piece in range(4):
            if piece < 3:
                far_next(piece + 1)
            settle(piece)
        far_wait(3, far_send)

    passing().wait_send()
    sent(2)

    @pl.when(core == 0)
    def _():
        own_out.wait()
        wait_blocks(2 * CHIPS - 1, out_send.at[0])
        wait_blocks(CHIPS - 1, out_recv.at[0])

    @pl.when(core == 1)
    def _():
        wait_blocks(CHIPS, out_recv.at[0])

        @pl.when(side == group)
        def _():
            own_out.wait()
            wait_blocks(2 * CHIPS - 1, out_send.at[1])

        @pl.when(side != group)
        def _():
            wait_blocks(2 * CHIPS, out_send.at[1])

    @pl.when(jnp.logical_and(core == 1, side == group))
    def _():
        wait_blocks(CHIPS - 1, out_recv.at[1])

    @pl.when(jnp.logical_or(core == 0, side != group))
    def _():
        wait_blocks(CHIPS, out_recv.at[1])


def finish(landed, grad, skip, grad_in, filter_grad):
    channels = grad.shape[0]
    shape = (channels, skip.shape[1])
    chosen = lax.broadcasted_iota(jnp.int32, shape, 1) == (
        lax.broadcasted_iota(jnp.int32, shape, 0) + pl.program_id(0) * channels
    )
    gain = jnp.sum(jnp.where(chosen, skip[...], 0.0), axis=1, keepdims=True)
    for n in range(ROWS):
        at = slice(n * COLS, (n + 1) * COLS)
        grad_in[:, at] = landed[0, :, n, :] + gain * grad[:, at]
        filter_grad[:, at] = landed[1, :, n, :]


def shards(inputs, grad_out, filters, skip):
    channels, length = filters.shape
    constants = tables()
    vmem, dma = pltpu.VMEM, pltpu.SemaphoreType.DMA
    any_space = pl.BlockSpec(memory_space=pl.ANY)
    grad = grad_out.reshape(channels, length)
    landed = pl.pallas_call(
        kernel,
        out_shape=jax.ShapeDtypeStruct((2, CHIPS, ROWS, COLS), jnp.float32),
        in_specs=[any_space] * 8,
        out_specs=any_space,
        scratch_shapes=[
            vmem((3, channels, length), jnp.float32),
            vmem((3, CHIPS, ROWS, COLS), jnp.float32),
            vmem((2, CHIPS, 2, ROWS, COLS), jnp.float32),
            vmem((2, 2, 4, 4 * RAD, 2 * RAD), jnp.float32),
            vmem((2, 2, 4 * RAD, COLS), jnp.float32),
            vmem((2, 4, 2, 2 * RAD, COLS), jnp.bfloat16),
            vmem((CHIPS, 2, ROWS, COLS), jnp.float32),
            vmem((4, 4, 2, ROWS, COLS), jnp.float32),
            vmem(constants[0].shape, jnp.bfloat16),
            vmem(constants[1].shape, jnp.bfloat16),
            vmem(constants[2].shape, jnp.float32),
            vmem(constants[3].shape, jnp.bfloat16),
            vmem(constants[4].shape, jnp.bfloat16),
            dma((5,)), dma((3,)), dma((3,)), dma((3,)), dma((2,)), dma(()), dma(()), pltpu.SemaphoreType.REGULAR,
            dma((4,)), dma((4,)), dma((2,)), dma((2,)), dma(()),
        ],
        compiler_params=pltpu.CompilerParams(
            collective_id=0, has_side_effects=True, vmem_limit_bytes=56 * 2**20
        ),
        cost_estimate=pl.CostEstimate(flops=11 * 10**9, bytes_accessed=2 * 10**7, transcendentals=0),
    )(
        grad, inputs.reshape(channels, length), filters,
        *(jnp.asarray(table) for table in constants),
    )
    flat = pl.BlockSpec((16, length), lambda i: (i, 0))
    grad_in, filter_grad = pl.pallas_call(
        finish,
        out_shape=[jax.ShapeDtypeStruct((channels, length), jnp.float32)] * 2,
        grid=(channels // 16,),
        in_specs=[
            pl.BlockSpec((2, 16, ROWS, COLS), lambda i: (0, i, 0, 0)),
            flat,
            pl.BlockSpec((1, channels), lambda i: (0, 0)),
        ],
        out_specs=[flat, flat],
        cost_estimate=pl.CostEstimate(flops=10**6, bytes_accessed=5 * 2**20, transcendentals=0),
    )(landed, grad, skip.reshape(1, channels))
    return (grad_in.reshape(1, channels, length), filter_grad)


def solution(mesh):
    return jax.shard_map(
        shards,
        mesh=mesh,
        in_specs=(P("dp", None, "seq"), P("dp", None, "seq"), P(None, "seq"), P()),
        out_specs=(P("dp", None, "seq"), P(None, "seq")),
        check_vma=False,
    )
```
